128 devices in a mesh: tm: 8 (over y, core), hash: 16 (over z, x).
Axes of the slice: x: 4, y: 4, z: 4, core: 2. Of those that a mesh axis runs over, the one named last changes fastest.
Arguments:
- fact_blocks: bfloat16 [6144, 128, 128], P(('tm', 'hash'))
- owners: int32 [6144], P(('tm', 'hash')), may hold values from 0 to 15, as said below
- row_counts: int32 [6144], P(('tm', 'hash')), may hold values from 64 to 128
- neighbours: int32 [128, 16, 12], P(('tm', 'hash')), may hold values from 0 to 63
- entities: bfloat16 [1024, 128, 128], P('hash'), may hold values from -6 to 6
- col_gain: float32 [128], replicated, may hold values from 0.1 to 1.9
- w_self: bfloat16 [128, 512], replicated, may hold values from -0.5 to 0.5
- w_nbr: bfloat16 [128, 512], replicated, may hold values from -0.5 to 0.5
- mlp_bias: float32 [512], replicated, may hold values from -3 to 3
- w_mid: bfloat16 [512, 512], replicated, may hold values from -0.25 to 0.25
- w_out: bfloat16 [512, 128], replicated, may hold values from -0.25 to 0.25
Outputs:
- sage_out: bfloat16 [128, 96, 128, 128], P(('tm', 'hash'))
The draws below stay inside these ranges and needn't reach their ends.
Inputs may be any that keep to these rules, and one draw needn't show every extreme that they name: `owners`: each device sends at most 6 of its blocks to one owner; in every time partition one owner receives exactly 6 blocks from each of the 16 devices, and every owner receives at least one block.
All inputs are finite; a program needn't handle non-finite values.
Results may differ from the reference program's by a relative error of at most 0.011.
Values may be sent and summed in bfloat16 or wider, within the bound.
A program may use at most 128 MiB of HBM per device.

```python
import math
import jax
import jax.numpy as jnp
import numpy as np
from jax import lax

D = 128
HID = 512
ROWS = 128
KN = 2
B_DEV = 48
E_DEV = 64
TPARTS = 8
HOLDERS = 16
CAP = 6
Q = 12
SLOTS = 96
FACT_BLOCKS = 6144
ENT_BLOCKS = 1024
N_TM = 8
N_HASH = 16


def draw_fact_blocks(key, part):
    key_base = jax.random.fold_in(key, 11)
    key_col = jax.random.fold_in(key, 12)
    key_row = jax.random.fold_in(key, 13)
    col_scale = jnp.exp(jax.random.uniform(key_col, (D,), jnp.float32, 0.0, math.log(10.0)))
    row_scale = jnp.exp(jax.random.uniform(key_row, (FACT_BLOCKS, ROWS, 1), jnp.float32, 0.0, math.log(10.0)))
    period = jnp.arange(FACT_BLOCKS, dtype=jnp.int32) // (FACT_BLOCKS // TPARTS)
    base = jax.random.normal(key_base, (FACT_BLOCKS, ROWS, D), jnp.float32)
    growth = 3.0
    trend = growth ** (period.astype(jnp.float32) / (TPARTS - 1))
    return (base * col_scale * row_scale * trend[:, None, None]).astype(jnp.bfloat16)


def draw_owners(key, part):
    device_total = FACT_BLOCKS // B_DEV
    favored = jax.random.randint(jax.random.fold_in(key, 1), (TPARTS,), 0, HOLDERS)
    device_keys = jax.random.split(jax.random.fold_in(key, 2), device_total)
    heavy = jnp.repeat(favored, HOLDERS)
    assured_all = jnp.arange(device_total, dtype=jnp.int32) % HOLDERS % (HOLDERS - 1)

    def one_device(dev_key, chosen, assured):
        key_slots = jax.random.fold_in(dev_key, 3)
        key_order = jax.random.fold_in(dev_key, 4)
        drawn = jax.random.permutation(key_slots, (HOLDERS - 1) * CAP - 1)[:B_DEV - CAP - 1].astype(jnp.int32)
        drawn = jnp.where(drawn >= assured * CAP, drawn + 1, drawn)
        picked = jnp.concatenate([jnp.zeros((1,), jnp.int32) + assured, drawn // CAP]).astype(jnp.int32)
        others = jnp.where(picked >= chosen, picked + 1, picked).astype(jnp.int32)
        listed = jnp.concatenate([jnp.zeros((CAP,), jnp.int32) + chosen, others])
        return listed[jax.random.permutation(key_order, B_DEV)]
    return jax.vmap(one_device)(device_keys, heavy, assured_all).reshape(FACT_BLOCKS).astype(jnp.int32)


def with_ends(array, key, smallest, high):
    longest = array.shape.index(max(array.shape))
    spots = []
    for shift in (0, 1):
        where = [jax.random.randint(jax.random.fold_in(key, axis), (), 0, length) for axis, length in enumerate(array.shape)]
        where[longest] = (where[longest] + shift) % array.shape[longest]
        spots.append(tuple(where))
    return array.at[spots[0]].set(smallest).at[spots[1]].set(high)


def steps_of(rng, shape, shards, smallest, largest):
    level = 1.0
    for dim, blocks in shards:
        steps = jax.random.uniform(jax.random.fold_in(jax.random.fold_in(rng, 6), dim), (blocks,), jnp.float32, smallest / len(shards), largest / len(shards))
        level = level * jnp.repeat(jnp.exp(steps), shape[dim] // blocks).reshape((-1,) + (1,) * (len(shape) - 1 - dim))
    return level


def rank_bounds(amount, slope):
    portions = [(1 << 20) // math.isqrt(rank ** slope) + 1 for rank in range(1, amount + 1)]
    width = 1 + sum(portions) // (1 << 30)
    return np.cumsum(np.array([max(1, weight // width) for weight in portions]))


def skewed_ids(stream_key, shape, number_of, slope):
    table = rank_bounds(number_of, slope)
    ticket = jax.random.randint(jax.random.fold_in(stream_key, 1), shape, 0, int(table[number_of - 1]))
    rank = jnp.searchsorted(jnp.asarray(table, jnp.int32), ticket, side="right")
    return jax.random.permutation(jax.random.fold_in(stream_key, 2), number_of)[rank].astype(jnp.int32)


def noise(stream_key, shape, width, most, pieces=(), kind=jnp.bfloat16):
    loudness = steps_of(stream_key, shape, pieces, -0.22, 0.18) if pieces else 1.0
    values = jax.random.normal(stream_key, shape, jnp.float32) * width * loudness
    return jnp.minimum(jnp.maximum(values, -most), most).astype(kind)


def setup_inputs(seed: int = 0) -> dict:
    arg_keys = jax.random.split(jax.random.key(seed), 12)
    return {
        "fact_blocks": draw_fact_blocks(jax.random.fold_in(arg_keys[11], 71), 0),
        "owners": draw_owners(jax.random.fold_in(arg_keys[11], 71), 0),
        "row_counts": with_ends(jax.random.randint(arg_keys[2], (FACT_BLOCKS,), ROWS // 2, ROWS + 1), jax.random.fold_in(arg_keys[2], 1), ROWS // 2, ROWS).astype(jnp.int32),
        "neighbours": with_ends(skewed_ids(arg_keys[3], (N_TM * N_HASH, HOLDERS, Q), E_DEV, 2), jax.random.fold_in(arg_keys[3], 3), 0, E_DEV - 1).astype(jnp.int32),
        "entities": noise(arg_keys[4], (ENT_BLOCKS, ROWS, D), 1.0, 6.0, ((0, 16),)),
        "col_gain": jnp.clip(1.0 + 0.18 * jax.random.normal(arg_keys[5], (D,), jnp.float32), 0.1, 1.9),
        "w_self": noise(arg_keys[6], (D, HID), D ** -0.5, 0.5),
        "w_nbr": noise(arg_keys[7], (D, HID), D ** -0.5, 0.5),
        "mlp_bias": noise(arg_keys[8], (HID,), 0.5, 3.0, (), jnp.float32),
        "w_mid": noise(arg_keys[9], (HID, HID), HID ** -0.5, 0.25),
        "w_out": noise(arg_keys[10], (HID, D), HID ** -0.5, 0.25),
    }


def reference(fact_blocks, owners, row_counts, neighbours, entities, col_gain, w_self, w_nbr, mlp_bias, w_mid, w_out):
    groups = fact_blocks.reshape(N_TM, N_HASH, B_DEV, ROWS, D)
    owned = owners.reshape(N_TM, N_HASH, B_DEV)
    counted = row_counts.reshape(N_TM, N_HASH, B_DEV)

    def relay(packed):
        blocks_t, owned_t, counted_t = packed
        one_hot = (owned_t[..., None] == jnp.arange(N_HASH, dtype=jnp.int32)).astype(jnp.int32)
        ranking = lax.optimization_barrier(jnp.sum((jnp.cumsum(one_hot, axis=1) - 1) * one_hot, axis=2)).astype(jnp.int32)
        source = jnp.broadcast_to(jnp.arange(N_HASH, dtype=jnp.int32)[:, None], owned_t.shape)
        placed = jnp.zeros((N_HASH, N_HASH, CAP, ROWS, D), blocks_t.dtype).at[owned_t, source, ranking].set(blocks_t)
        slot_counts = jnp.zeros((N_HASH, N_HASH, CAP), jnp.int32).at[owned_t, source, ranking].set(counted_t)
        return (placed, slot_counts)
    placed, slot_counts = lax.map(relay, (groups, owned, counted))
    lists = neighbours.reshape(N_TM, N_HASH, N_HASH, Q)
    offsets = (jnp.arange(N_HASH, dtype=jnp.int32) * E_DEV)[None, :, None]

    def owner_layer(owner):
        blocks_h = placed[:, owner].reshape(N_TM, SLOTS, ROWS, D).astype(jnp.float32)
        counts_h = slot_counts[:, owner].reshape(N_TM, SLOTS)
        valid = (jnp.arange(ROWS, dtype=jnp.int32)[None, None, :] < counts_h[..., None]).astype(jnp.float32)
        col_sum = jnp.einsum('tsr,tsrd->d', valid, blocks_h)
        col_sq = jnp.einsum('tsr,tsrd->d', valid, blocks_h * blocks_h)
        live = jnp.sum(valid)
        col_mean = col_sum / live
        col_var = col_sq / live - col_mean * col_mean
        normed = ((blocks_h - col_mean) * lax.rsqrt(col_var + 1e-05) * col_gain).astype(jnp.bfloat16)
        index = (lists[:, owner] + offsets).astype(jnp.int32)
        found = entities[index].astype(jnp.float32).reshape(N_TM, N_HASH, CAP, KN, ROWS, D)
        agg = (lax.optimization_barrier(jnp.sum(found, axis=3)) * (1.0 / KN)).astype(jnp.bfloat16).reshape(N_TM * SLOTS * ROWS, D)
        flat = normed.reshape(N_TM * SLOTS * ROWS, D)
        first = jnp.dot(flat, w_self, preferred_element_type=jnp.float32) + jnp.dot(agg, w_nbr, preferred_element_type=jnp.float32) + mlp_bias
        hidden_one = jnp.maximum(first, 0.0).astype(jnp.bfloat16)
        hidden_two = jnp.maximum(jnp.dot(hidden_one, w_mid, preferred_element_type=jnp.float32), 0.0).astype(jnp.bfloat16)
        result = jnp.dot(hidden_two, w_out, preferred_element_type=jnp.float32) * valid.reshape(-1, 1)
        return result.astype(jnp.bfloat16).reshape(N_TM, SLOTS, ROWS, D)
    stacked = lax.map(owner_layer, jnp.arange(N_HASH, dtype=jnp.int32))
    return jnp.transpose(stacked, (1, 0, 2, 3, 4)).reshape(N_TM * N_HASH, SLOTS, ROWS, D)
```

```python
import functools

import jax
import jax.numpy as jnp
from jax import lax
from jax.experimental import pallas as pl
from jax.experimental.pallas import tpu as pltpu
from jax.sharding import PartitionSpec as P

MESH = pl.DeviceIdType.MESH
HOLD = 16
TM = 8
CAP = 6
B = 48
R = 128
D = 128
HID = 512
EPS = 1e-05
CHUNKS = 4
F32 = jnp.float32
BF16 = jnp.bfloat16


def peer(s, dz, dx):
    return lax.rem(lax.div(s, 4) + dz, 4) * 4 + lax.rem(lax.rem(s, 4) + dx, 4)


def kernel(
    fact_hbm, own_v, cnt_v, cnt_s, nb_v, ent_hbm, gain_v, wself_hbm, wnbr_hbm, bias_v, wmid_hbm, wout_hbm,
    o_ref,
    facts, ent, w1, wmid, wout, bs, bq, st, r1, r2, fin, nbs, rnb, tab_v, nbt_v, tab_s, nb_s, mean_v, scale_v,
    in1, send, lsem, s1, q1, s2, q2, s3, q3, sn, qn, ss, qs,
):
    t = lax.axis_index("tm")
    s = lax.axis_index("hash")

    bar = pltpu.get_barrier_semaphore()
    for i in range(1, TM):
        pl.semaphore_signal(bar, inc=1, device_id={"tm": lax.rem(t + i, TM)}, device_id_type=MESH)
    for d in range(1, HOLD):
        pl.semaphore_signal(bar, inc=1, device_id={"hash": peer(s, d // 4, d % 4)}, device_id_type=MESH)

    per = B // CHUNKS
    loads = [
        pltpu.make_async_copy(fact_hbm.at[pl.ds(k * per, per)], facts.at[pl.ds(k * per, per)], lsem.at[k])
        for k in range(CHUNKS)
    ]
    rest = [
        pltpu.make_async_copy(wself_hbm, w1.at[pl.ds(0, D)], lsem.at[CHUNKS]),
        pltpu.make_async_copy(wnbr_hbm, w1.at[pl.ds(D, D)], lsem.at[CHUNKS + 1]),
        pltpu.make_async_copy(wmid_hbm, wmid, lsem.at[CHUNKS + 2]),
        pltpu.make_async_copy(wout_hbm, wout, lsem.at[CHUNKS + 3]),
        pltpu.make_async_copy(ent_hbm, ent, lsem.at[CHUNKS + 4]),
    ]
    for cp in loads + rest:
        cp.start()

    hot = (lax.broadcasted_iota(jnp.int32, (HOLD, B), 0) == own_v[...]).astype(F32)
    upper = (
        lax.broadcasted_iota(jnp.int32, (B, B), 0) <= lax.broadcasted_iota(jnp.int32, (B, B), 1)
    ).astype(BF16)
    order = jnp.dot(hot.astype(BF16), upper, preferred_element_type=F32)
    cnt = cnt_v[...].astype(F32)
    blk = lax.broadcasted_iota(jnp.int32, (HOLD, B), 1).astype(F32)
    lane = lax.broadcasted_iota(jnp.int32, (HOLD, 128), 1)
    tab = jnp.zeros((HOLD, 128), F32)
    for c in range(CAP):
        sel = jnp.where(order == float(c + 1), hot, 0.0)
        tab = jnp.where(lane == c, jnp.sum(sel * blk, axis=1, keepdims=True), tab)
        tab = jnp.where(lane == 8 + c, jnp.sum(sel * cnt, axis=1, keepdims=True), tab)
    tab_v[...] = tab.astype(jnp.int32)
    tab_copy = pltpu.make_async_copy(tab_v, tab_s, lsem.at[CHUNKS + 5])
    tab_copy.start()

    nbs[...] = jnp.zeros_like(nbs)
    nbt_v[...] = jnp.zeros_like(nbt_v)
    for q in range(2 * CAP):
        nbt_v[q : q + 1, 0:HOLD] = nb_v[q]
    lists = nbt_v[...].T
    for j in range(HOLD):
        nbs[j, 0:1, 0:HOLD] = lists[j : j + 1, :]

    row = lax.broadcasted_iota(jnp.int32, (R, D), 0)
    for k in range(CHUNKS):
        loads[k].wait()

        def stat(i, carry):
            for j in range(2):
                b = k * per + i * 2 + j
                x = jnp.where(row < cnt_s[b], facts[b].astype(F32), 0.0)
                bs[pl.ds(b, 1), :] = jnp.sum(x, axis=0, keepdims=True)
                bq[pl.ds(b, 1), :] = jnp.sum(x * x, axis=0, keepdims=True)
            return carry

        lax.fori_loop(0, per // 2, stat, 0)
    sums = jnp.dot(hot, bs[...], preferred_element_type=F32, precision=lax.Precision.HIGHEST)
    squares = jnp.dot(hot, bq[...], preferred_element_type=F32, precision=lax.Precision.HIGHEST)
    live = jnp.broadcast_to(jnp.sum(hot * cnt, axis=1, keepdims=True), (HOLD, 128))
    st[...] = jnp.zeros_like(st)
    for h in range(HOLD):
        base = 3 * (h % 2)
        st[h // 2, base : base + 1, :] = sums[h : h + 1, :]
        st[h // 2, base + 1 : base + 2, :] = squares[h : h + 1, :]
        st[h // 2, base + 2 : base + 3, :] = live[h : h + 1, :]

    pl.semaphore_wait(bar, TM - 1 + HOLD - 1)

    first = []
    for i in range(1, TM):
        p = lax.rem(t + i, TM)
        first.append(
            pltpu.make_async_remote_copy(
                src_ref=st.at[p], dst_ref=r1.at[t], send_sem=s1.at[i], recv_sem=q1.at[i],
                device_id={"tm": p}, device_id_type=MESH,
            )
        )
        first[-1].start()
    asks = []
    for d in range(1, HOLD):
        p = peer(s, d // 4, d % 4)
        asks.append(
            pltpu.make_async_remote_copy(
                src_ref=nbs.at[p], dst_ref=rnb.at[s], send_sem=sn.at[d], recv_sem=qn.at[d],
                device_id={"hash": p}, device_id_type=MESH,
            )
        )
        asks[-1].start()
    rnb[s] = nbs[s]
    r1[t] = st[t]
    for cp in first:
        cp.wait_recv()
    r2[s] = jnp.sum(r1[...], axis=0)
    second = []
    for d in range(1, HOLD):
        p = peer(s, d // 4, d % 4)
        second.append(
            pltpu.make_async_remote_copy(
                src_ref=r2.at[s], dst_ref=r2.at[s], send_sem=s2.at[d], recv_sem=q2.at[d],
                device_id={"hash": p}, device_id_type=MESH,
            )
        )
        second[-1].start()
    for cp in asks:
        cp.wait_recv()
    for h in range(HOLD):
        nbt_v[h : h + 1, :] = rnb[h, 0:1, :]
    nb_copy = pltpu.make_async_copy(nbt_v, nb_s, lsem.at[CHUNKS + 6])
    nb_copy.start()
    for cp in rest:
        cp.wait()
    for cp in second:
        cp.wait_recv()
    fin[t] = jnp.sum(r2[...], axis=0)
    third = []
    for i in range(1, TM):
        p = lax.rem(t + i, TM)
        third.append(
            pltpu.make_async_remote_copy(
                src_ref=fin.at[t], dst_ref=fin.at[t], send_sem=s3.at[i], recv_sem=q3.at[i],
                device_id={"tm": p}, device_id_type=MESH,
            )
        )
        third[-1].start()
    tab_copy.wait()
    nb_copy.wait()
    for cp in third:
        cp.wait_recv()
    for h in range(HOLD):
        base = 3 * (h % 2)
        n = fin[h // 2, base + 2 : base + 3, :]
        mean = fin[h // 2, base : base + 1, :] / n
        var = fin[h // 2, base + 1 : base + 2, :] / n - mean * mean
        mean_v[h : h + 1, :] = mean
        scale_v[h : h + 1, :] = lax.rsqrt(var + EPS) * gain_v[...]

    def copy_of(dz, dx, c):
        k = (dz * 4 + dx) * CAP + c
        return pltpu.make_async_remote_copy(
            src_ref=send.at[k], dst_ref=o_ref.at[s * CAP + c], send_sem=ss.at[k], recv_sem=qs.at[k],
            device_id={"hash": peer(s, dz, dx)}, device_id_type=MESH,
        )

    def step(n, carry):
        c, dz = lax.div(n, 4), lax.rem(n, 4)
        for dx in range(4):
            p = peer(s, dz, dx)
            x = facts[jnp.clip(tab_s[p, c], 0, B - 1)].astype(F32)
            x = (x - mean_v[pl.ds(p, 1), :]) * scale_v[pl.ds(p, 1), :]
            in1[dx * R : (dx + 1) * R, 0:D] = x.astype(BF16)
            e = ent[nb_s[p, 2 * c]].astype(F32) + ent[nb_s[p, 2 * c + 1]].astype(F32)
            in1[dx * R : (dx + 1) * R, D : 2 * D] = (e * 0.5).astype(BF16)
        h1 = jnp.dot(in1[...], w1[...], preferred_element_type=F32) + bias_v[...]
        h1 = jnp.maximum(h1, 0.0).astype(BF16)
        h2 = jnp.dot(h1, wmid[...], preferred_element_type=F32)
        h2 = jnp.maximum(h2, 0.0).astype(BF16)
        out = jnp.dot(h2, wout[...], preferred_element_type=F32)
        for dx in range(4):
            p = peer(s, dz, dx)
            y = jnp.where(row < tab_s[p, 8 + c], out[dx * R : (dx + 1) * R, :], 0.0).astype(BF16)
            send[(dz * 4 + dx) * CAP + c] = y
            if dx:
                copy_of(dz, dx, c).start()
            else:

                @pl.when(dz > 0)
                def _():
                    copy_of(dz, 0, c).start()

                @pl.when(dz == 0)
                def _():
                    o_ref[s * CAP + c] = y

        return carry

    lax.fori_loop(0, 4 * CAP, step, 0)

    for cp in first + asks + second + third:
        cp.wait_send()

    def finish(k, carry):
        d, c = lax.div(k, CAP) + 1, lax.rem(k, CAP)
        copy_of(lax.div(d, 4), lax.rem(d, 4), c).wait()
        return carry

    lax.fori_loop(0, (HOLD - 1) * CAP, finish, 0)


def body(fact_blocks, owners, row_counts, neighbours, entities, col_gain, w_self, w_nbr, mlp_bias, w_mid, w_out):
    vmem = pl.BlockSpec(memory_space=pltpu.VMEM)
    smem = pl.BlockSpec(memory_space=pltpu.SMEM)
    hbm = pl.BlockSpec(memory_space=pl.ANY)
    dma = pltpu.SemaphoreType.DMA
    out = pl.pallas_call(
        kernel,
        out_shape=jax.ShapeDtypeStruct((HOLD * CAP, R, D), BF16),
        in_specs=[hbm, vmem, vmem, smem, vmem, hbm, vmem, hbm, hbm, vmem, hbm, hbm],
        out_specs=vmem,
        scratch_shapes=[
            pltpu.VMEM((B, R, D), BF16),
            pltpu.VMEM((64, R, D), BF16),
            pltpu.VMEM((2 * D, HID), BF16),
            pltpu.VMEM((HID, HID), BF16),
            pltpu.VMEM((HID, D), BF16),
            pltpu.VMEM((B, D), F32),
            pltpu.VMEM((B, D), F32),
            pltpu.VMEM((TM, 8, 128), F32),
            pltpu.VMEM((TM, 8, 128), F32),
            pltpu.VMEM((HOLD, 8, 128), F32),
            pltpu.VMEM((TM, 8, 128), F32),
            pltpu.VMEM((HOLD, 8, 128), jnp.int32),
            pltpu.VMEM((HOLD, 8, 128), jnp.int32),
            pltpu.VMEM((HOLD, 128), jnp.int32),
            pltpu.VMEM((HOLD, 128), jnp.int32),
            pltpu.SMEM((HOLD, 128), jnp.int32),
            pltpu.SMEM((HOLD, 128), jnp.int32),
            pltpu.VMEM((HOLD, D), F32),
            pltpu.VMEM((HOLD, D), F32),
            pltpu.VMEM((4 * R, 2 * D), BF16),
            pltpu.VMEM((HOLD * CAP, R, D), BF16),
            dma((CHUNKS + 7,)),
            dma((TM,)), dma((TM,)),
            dma((HOLD,)), dma((HOLD,)),
            dma((TM,)), dma((TM,)),
            dma((HOLD,)), dma((HOLD,)),
            dma((HOLD * CAP,)), dma((HOLD * CAP,)),
        ],
        compiler_params=pltpu.CompilerParams(
            collective_id=0, has_side_effects=True, vmem_limit_bytes=60 << 20
        ),
        cost_estimate=pl.CostEstimate(flops=12 * 10**9, bytes_accessed=10 * 2**20, transcendentals=0),
    )(
        fact_blocks,
        owners.reshape(1, B),
        row_counts.reshape(1, B),
        row_counts,
        neighbours.transpose(2, 0, 1),
        entities,
        col_gain.reshape(1, D),
        w_self,
        w_nbr,
        mlp_bias.reshape(1, HID),
        w_mid,
        w_out,
    )
    return out[None]


def solution(mesh):
    return jax.shard_map(
        body,
        mesh=mesh,
        in_specs=(
            P(("tm", "hash"), None, None),
            P(("tm", "hash")),
            P(("tm", "hash")),
            P(("tm", "hash"), None, None),
            P("hash", None, None),
            P(),
            P(),
            P(),
            P(),
            P(),
            P(),
        ),
        out_specs=P(("tm", "hash"), None, None, None),
        check_vma=False,
    )
```

```python
import functools

import jax
import jax.numpy as jnp
from jax import lax
from jax.experimental import pallas as pl
from jax.experimental.pallas import tpu as pltpu
from jax.sharding import PartitionSpec as P

MESH = pl.DeviceIdType.MESH
HOLD = 16
TM = 8
CAP = 6
B = 48
R = 128
D = 128
HID = 512
EPS = 1e-05
CHUNKS = 4
F32 = jnp.float32
BF16 = jnp.bfloat16


def peer(s, dz, dx):
    return lax.rem(lax.div(s, 4) + dz, 4) * 4 + lax.rem(lax.rem(s, 4) + dx, 4)


def kernel(
    fact_hbm, own_v, cnt_v, cnt_s, nb_v, ent_hbm, gain_v, wself_hbm, wnbr_hbm, bias_v, wmid_hbm, wout_hbm,
    o_ref,
    facts, ent, w1, wmid, wout, bs, bq, st, r1, r2, fin, nbs, rnb, wide, tab_v, nbt_v, tab_s, nb_s, mean_v, scale_v,
    in1, send, xs, ags, ex, ea, lsem, s1, q1, s2, q2, s3, q3, sn, qn, sx, qx, sa, qa, ss, qs,
):
    t = lax.axis_index("tm")
    s = lax.axis_index("hash")

    bar = pltpu.get_barrier_semaphore()
    for i in range(1, TM):
        pl.semaphore_signal(bar, inc=1, device_id={"tm": lax.rem(t + i, TM)}, device_id_type=MESH)
    for d in range(1, HOLD):
        pl.semaphore_signal(bar, inc=1, device_id={"hash": peer(s, d // 4, d % 4)}, device_id_type=MESH)

    per = B // CHUNKS
    loads = [
        pltpu.make_async_copy(fact_hbm.at[pl.ds(k * per, per)], facts.at[pl.ds(k * per, per)], lsem.at[k])
        for k in range(CHUNKS)
    ]
    rest = [
        pltpu.make_async_copy(wself_hbm, w1.at[pl.ds(0, D)], lsem.at[CHUNKS]),
        pltpu.make_async_copy(wnbr_hbm, w1.at[pl.ds(D, D)], lsem.at[CHUNKS + 1]),
        pltpu.make_async_copy(wmid_hbm, wmid, lsem.at[CHUNKS + 2]),
        pltpu.make_async_copy(wout_hbm, wout, lsem.at[CHUNKS + 3]),
        pltpu.make_async_copy(ent_hbm, ent, lsem.at[CHUNKS + 4]),
    ]
    for cp in loads + rest:
        cp.start()

    hot = (lax.broadcasted_iota(jnp.int32, (HOLD, B), 0) == own_v[...]).astype(F32)
    upper = (
        lax.broadcasted_iota(jnp.int32, (B, B), 0) <= lax.broadcasted_iota(jnp.int32, (B, B), 1)
    ).astype(BF16)
    order = jnp.dot(hot.astype(BF16), upper, preferred_element_type=F32)
    cnt = cnt_v[...].astype(F32)
    blk = lax.broadcasted_iota(jnp.int32, (HOLD, B), 1).astype(F32)
    lane = lax.broadcasted_iota(jnp.int32, (HOLD, 128), 1)
    tab = jnp.zeros((HOLD, 128), F32)
    for c in range(CAP):
        sel = jnp.where(order == float(c + 1), hot, 0.0)
        tab = jnp.where(lane == c, jnp.sum(sel * blk, axis=1, keepdims=True), tab)
        tab = jnp.where(lane == 16 + c, jnp.sum(sel * cnt, axis=1, keepdims=True), tab)
    tab_v[...] = tab.astype(jnp.int32)
    tab_copy = pltpu.make_async_copy(tab_v, tab_s, lsem.at[CHUNKS + 5])
    tab_copy.start()

    wide[...] = jnp.zeros_like(wide)
    for q in range(2 * CAP):
        wide[q : q + 1, 0:HOLD] = nb_v[q]
    note = jnp.where(lane < 16, wide[...].T[0:HOLD, :], tab_v[...])
    for j in range(HOLD):
        nbs[j] = note[j : j + 1, :]

    row = lax.broadcasted_iota(jnp.int32, (R, D), 0)
    for k in range(CHUNKS):
        loads[k].wait()

        def stat(i, carry):
            for j in range(2):
                b = k * per + i * 2 + j
                x = jnp.where(row < cnt_s[b], facts[b].astype(F32), 0.0)
                bs[pl.ds(b, 1), :] = jnp.sum(x, axis=0, keepdims=True)
                bq[pl.ds(b, 1), :] = jnp.sum(x * x, axis=0, keepdims=True)
            return carry

        lax.fori_loop(0, per // 2, stat, 0)
    sums = jnp.dot(hot, bs[...], preferred_element_type=F32, precision=lax.Precision.HIGHEST)
    squares = jnp.dot(hot, bq[...], preferred_element_type=F32, precision=lax.Precision.HIGHEST)
    live = jnp.broadcast_to(jnp.sum(hot * cnt, axis=1, keepdims=True), (HOLD, 128))
    st[...] = jnp.zeros_like(st)
    for h in range(HOLD):
        base = 3 * (h % 2)
        st[h // 2, base : base + 1, :] = sums[h : h + 1, :]
        st[h // 2, base + 1 : base + 2, :] = squares[h : h + 1, :]
        st[h // 2, base + 2 : base + 3, :] = live[h : h + 1, :]

    tab_copy.wait()
    for d in range(HOLD):
        p = peer(s, d // 4, d % 4)
        x = facts[jnp.clip(tab_s[p, CAP - 1], 0, B - 1)]
        if d:
            xs[p] = x
        else:
            ex[s] = x

    pl.semaphore_wait(bar, TM - 1 + HOLD - 1)

    first = []
    for i in range(1, TM):
        p = lax.rem(t + i, TM)
        first.append(
            pltpu.make_async_remote_copy(
                src_ref=st.at[p], dst_ref=r1.at[t], send_sem=s1.at[i], recv_sem=q1.at[i],
                device_id={"tm": p}, device_id_type=MESH,
            )
        )
        first[-1].start()
    asks = []
    for d in range(1, HOLD):
        p = peer(s, d // 4, d % 4)
        asks.append(
            pltpu.make_async_remote_copy(
                src_ref=nbs.at[p], dst_ref=rnb.at[s], send_sem=sn.at[d], recv_sem=qn.at[d],
                device_id={"hash": p}, device_id_type=MESH,
            )
        )
        asks[-1].start()
    early = []
    for d in range(1, HOLD):
        p = peer(s, d // 4, d % 4)
        early.append(
            pltpu.make_async_remote_copy(
                src_ref=xs.at[p], dst_ref=ex.at[s], send_sem=sx.at[d], recv_sem=qx.at[d],
                device_id={"hash": p}, device_id_type=MESH,
            )
        )
        early[-1].start()
    rnb[s] = nbs[s]
    r1[t] = st[t]
    for cp in first:
        cp.wait_recv()
    r2[s] = jnp.sum(r1[...], axis=0)
    second = []
    for d in range(1, HOLD):
        p = peer(s, d // 4, d % 4)
        second.append(
            pltpu.make_async_remote_copy(
                src_ref=r2.at[s], dst_ref=r2.at[s], send_sem=s2.at[d], recv_sem=q2.at[d],
                device_id={"hash": p}, device_id_type=MESH,
            )
        )
        second[-1].start()
    for cp in asks:
        cp.wait_recv()
    for h in range(HOLD):
        nbt_v[h : h + 1, :] = rnb[h]
    nb_copy = pltpu.make_async_copy(nbt_v, nb_s, lsem.at[CHUNKS + 6])
    nb_copy.start()
    for cp in rest:
        cp.wait()
    nb_copy.wait()

    def agg_of(p, c):
        e = ent[nb_s[p, 2 * c]].astype(F32) + ent[nb_s[p, 2 * c + 1]].astype(F32)
        return (e * 0.5).astype(BF16)

    for d in range(HOLD):
        p = peer(s, d // 4, d % 4)
        if d:
            ags[p] = agg_of(p, CAP - 1)
            early.append(
                pltpu.make_async_remote_copy(
                    src_ref=ags.at[p], dst_ref=ea.at[s], send_sem=sa.at[d], recv_sem=qa.at[d],
                    device_id={"hash": p}, device_id_type=MESH,
                )
            )
            early[-1].start()
        else:
            ea[s] = agg_of(p, CAP - 1)
    for cp in second:
        cp.wait_recv()
    fin[t] = jnp.sum(r2[...], axis=0)
    third = []
    for i in range(1, TM):
        p = lax.rem(t + i, TM)
        third.append(
            pltpu.make_async_remote_copy(
                src_ref=fin.at[t], dst_ref=fin.at[t], send_sem=s3.at[i], recv_sem=q3.at[i],
                device_id={"tm": p}, device_id_type=MESH,
            )
        )
        third[-1].start()
    for cp in third:
        cp.wait_recv()
    for h in range(HOLD):
        base = 3 * (h % 2)
        n = fin[h // 2, base + 2 : base + 3, :]
        mean = fin[h // 2, base : base + 1, :] / n
        var = fin[h // 2, base + 1 : base + 2, :] / n - mean * mean
        mean_v[h : h + 1, :] = mean
        scale_v[h : h + 1, :] = lax.rsqrt(var + EPS) * gain_v[...]

    def copy_of(dz, dx, c):
        k = (dz * 4 + dx) * CAP + c
        return pltpu.make_async_remote_copy(
            src_ref=send.at[k], dst_ref=o_ref.at[s * CAP + c], send_sem=ss.at[k], recv_sem=qs.at[k],
            device_id={"hash": peer(s, dz, dx)}, device_id_type=MESH,
        )

    def own_copy(c):
        return pltpu.make_async_copy(send.at[c], o_ref.at[s * CAP + c], ss.at[c])

    def norm_of(x, p):
        x = (x.astype(F32) - mean_v[pl.ds(p, 1), :]) * scale_v[pl.ds(p, 1), :]
        return x.astype(BF16)

    def layers():
        h1 = jnp.dot(in1[...], w1[...], preferred_element_type=F32) + bias_v[...]
        h1 = jnp.maximum(h1, 0.0).astype(BF16)
        h2 = jnp.dot(h1, wmid[...], preferred_element_type=F32)
        h2 = jnp.maximum(h2, 0.0).astype(BF16)
        return jnp.dot(h2, wout[...], preferred_element_type=F32)

    def step(n, carry):
        c, dz = lax.div(n, 4), lax.rem(n, 4)
        for dx in range(4):
            p = peer(s, dz, dx)
            in1[dx * R : (dx + 1) * R, 0:D] = norm_of(facts[jnp.clip(tab_s[p, c], 0, B - 1)], p)
            in1[dx * R : (dx + 1) * R, D : 2 * D] = agg_of(p, c)
        out = layers()
        for dx in range(4):
            p = peer(s, dz, dx)
            y = jnp.where(row < tab_s[p, 16 + c], out[dx * R : (dx + 1) * R, :], 0.0)
            send[(dz * 4 + dx) * CAP + c] = y.astype(BF16)
            if dx:
                copy_of(dz, dx, c).start()
            else:

                @pl.when(dz > 0)
                def _():
                    copy_of(dz, 0, c).start()

                @pl.when(dz == 0)
                def _():
                    own_copy(c).start()

        return carry

    lax.fori_loop(0, 4 * (CAP - 1), step, 0)

    for cp in early:
        cp.wait_recv()

    def late_copy(k):
        return pltpu.make_async_copy(ea.at[k], o_ref.at[k * CAP + CAP - 1], ss.at[k * CAP + CAP - 1])

    def late(n, carry):
        for i in range(4):
            k = n * 4 + i
            in1[i * R : (i + 1) * R, 0:D] = norm_of(ex[k], s)
            in1[i * R : (i + 1) * R, D : 2 * D] = ea[k]
        out = layers()
        for i in range(4):
            k = n * 4 + i
            y = jnp.where(row < nb_s[k, 16 + CAP - 1], out[i * R : (i + 1) * R, :], 0.0)
            ea[k] = y.astype(BF16)
            late_copy(k).start()
        return carry

    lax.fori_loop(0, HOLD // 4, late, 0)

    for cp in first + asks + second + third + early:
        cp.wait_send()
    for c in range(CAP - 1):
        own_copy(c).wait()
    for k in range(HOLD):
        late_copy(k).wait()

    def finish(k, carry):
        d, c = lax.div(k, CAP - 1) + 1, lax.rem(k, CAP - 1)
        copy_of(lax.div(d, 4), lax.rem(d, 4), c).wait()
        return carry

    lax.fori_loop(0, (HOLD - 1) * (CAP - 1), finish, 0)


def body(fact_blocks, owners, row_counts, neighbours, entities, col_gain, w_self, w_nbr, mlp_bias, w_mid, w_out):
    vmem = pl.BlockSpec(memory_space=pltpu.VMEM)
    smem = pl.BlockSpec(memory_space=pltpu.SMEM)
    hbm = pl.BlockSpec(memory_space=pl.ANY)
    dma = pltpu.SemaphoreType.DMA
    out = pl.pallas_call(
        kernel,
        out_shape=jax.ShapeDtypeStruct((HOLD * CAP, R, D), BF16),
        in_specs=[hbm, vmem, vmem, smem, vmem, hbm, vmem, hbm, hbm, vmem, hbm, hbm],
        out_specs=hbm,
        scratch_shapes=[
            pltpu.VMEM((B, R, D), BF16),
            pltpu.VMEM((64, R, D), BF16),
            pltpu.VMEM((2 * D, HID), BF16),
            pltpu.VMEM((HID, HID), BF16),
            pltpu.VMEM((HID, D), BF16),
            pltpu.VMEM((B, D), F32),
            pltpu.VMEM((B, D), F32),
            pltpu.VMEM((TM, 8, 128), F32),
            pltpu.VMEM((TM, 8, 128), F32),
            pltpu.VMEM((HOLD, 8, 128), F32),
            pltpu.VMEM((TM, 8, 128), F32),
            pltpu.VMEM((HOLD, 1, 128), jnp.int32),
            pltpu.VMEM((HOLD, 1, 128), jnp.int32),
            pltpu.VMEM((128, 128), jnp.int32),
            pltpu.VMEM((HOLD, 128), jnp.int32),
            pltpu.VMEM((HOLD, 128), jnp.int32),
            pltpu.SMEM((HOLD, 128), jnp.int32),
            pltpu.SMEM((HOLD, 128), jnp.int32),
            pltpu.VMEM((HOLD, D), F32),
            pltpu.VMEM((HOLD, D), F32),
            pltpu.VMEM((4 * R, 2 * D), BF16),
            pltpu.VMEM((HOLD * CAP, R, D), BF16),
            pltpu.VMEM((HOLD, R, D), BF16),
            pltpu.VMEM((HOLD, R, D), BF16),
            pltpu.VMEM((HOLD, R, D), BF16),
            pltpu.VMEM((HOLD, R, D), BF16),
            dma((CHUNKS + 7,)),
            dma((TM,)), dma((TM,)),
            dma((HOLD,)), dma((HOLD,)),
            dma((TM,)), dma((TM,)),
            dma((HOLD,)), dma((HOLD,)),
            dma((HOLD,)), dma((HOLD,)),
            dma((HOLD,)), dma((HOLD,)),
            dma((HOLD * CAP,)), dma((HOLD * CAP,)),
        ],
        compiler_params=pltpu.CompilerParams(
            collective_id=0, has_side_effects=True, vmem_limit_bytes=60 << 20
        ),
        cost_estimate=pl.CostEstimate(flops=12 * 10**9, bytes_accessed=10 * 2**20, transcendentals=0),
    )(
        fact_blocks,
        owners.reshape(1, B),
        row_counts.reshape(1, B),
        row_counts,
        neighbours.transpose(2, 0, 1),
        entities,
        col_gain.reshape(1, D),
        w_self,
        w_nbr,
        mlp_bias.reshape(1, HID),
        w_mid,
        w_out,
    )
    return out[None]


def solution(mesh):
    return jax.shard_map(
        body,
        mesh=mesh,
        in_specs=(
            P(("tm", "hash"), None, None),
            P(("tm", "hash")),
            P(("tm", "hash")),
            P(("tm", "hash"), None, None),
            P("hash", None, None),
            P(),
            P(),
            P(),
            P(),
            P(),
            P(),
        ),
        out_specs=P(("tm", "hash"), None, None, None),
        check_vma=False,
    )
```

```python
import functools

import jax
import jax.numpy as jnp
from jax import lax
from jax.experimental import pallas as pl
from jax.experimental.pallas import tpu as pltpu
from jax.sharding import PartitionSpec as P

MESH = pl.DeviceIdType.MESH
HOLD = 16
TM = 8
CAP = 6
B = 48
R = 128
D = 128
HID = 512
EPS = 1e-05
CHUNKS = 4
F32 = jnp.float32
BF16 = jnp.bfloat16


def peer(s, dz, dx):
    return lax.rem(lax.div(s, 4) + dz, 4) * 4 + lax.rem(lax.rem(s, 4) + dx, 4)


def kernel(
    fact_hbm, own_hbm, cnt_hbm, cnt1_hbm, nb_hbm, ent_hbm, gain_hbm, wself_hbm, wnbr_hbm, bias_hbm, wmid_hbm, wout_hbm,
    o_ref,
    own_v, cnt_v, cnt_s, nb_v, gain_v, bias_v, facts, ent, w1, wmid, wout, bs, bq, st, r1, r2, fin, nbs, rnb, wide, tab_v, nbt_v, tab_s, nb_s, mean_v, scale_v,
    in1, send, xs, ags, ex, ea, lsem, s1, q1, s2, q2, s3, q3, sn, qn, sx, qx, sa, qa, ss, qs, tsem,
):
    t = lax.axis_index("tm")
    s = lax.axis_index("hash")

    bar = pltpu.get_barrier_semaphore()
    for i in range(1, TM):
        pl.semaphore_signal(bar, inc=1, device_id={"tm": lax.rem(t + i, TM)}, device_id_type=MESH)
    for d in range(1, HOLD):
        pl.semaphore_signal(bar, inc=1, device_id={"hash": peer(s, d // 4, d % 4)}, device_id_type=MESH)

    def group(src, dst, n, send_sem, recv_sem):
        return pltpu.make_async_remote_copy(
            src_ref=src.at[pl.ds(0, n)], dst_ref=dst.at[pl.ds(0, n)], send_sem=send_sem.at[0],
            recv_sem=recv_sem.at[0], device_id={"hash": peer(s, 0, 1)}, device_id_type=MESH,
        )

    first = group(st, r1, TM - 1, s1, q1)
    asks = group(nbs, rnb, HOLD - 1, sn, qn)
    second = group(r2, r2, HOLD - 1, s2, q2)
    third = group(fin, fin, TM - 1, s3, q3)
    early_x = group(xs, ex, HOLD - 1, sx, qx)
    early_a = group(ags, ea, HOLD - 1, sa, qa)
    rows_out = group(send, o_ref, (HOLD - 1) * (CAP - 1), ss, qs)

    per = B // CHUNKS
    loads = [
        pltpu.make_async_copy(fact_hbm.at[pl.ds(k * per, per)], facts.at[pl.ds(k * per, per)], lsem.at[k])
        for k in range(CHUNKS)
    ]
    rest = [
        pltpu.make_async_copy(wself_hbm, w1.at[pl.ds(0, D)], lsem.at[CHUNKS]),
        pltpu.make_async_copy(wnbr_hbm, w1.at[pl.ds(D, D)], lsem.at[CHUNKS + 1]),
        pltpu.make_async_copy(wmid_hbm, wmid, lsem.at[CHUNKS + 2]),
        pltpu.make_async_copy(wout_hbm, wout, lsem.at[CHUNKS + 3]),
        pltpu.make_async_copy(ent_hbm, ent, lsem.at[CHUNKS + 4]),
    ]
    tables = [
        pltpu.make_async_copy(own_hbm, own_v, tsem.at[0]),
        pltpu.make_async_copy(cnt_hbm, cnt_v, tsem.at[1]),
        pltpu.make_async_copy(cnt1_hbm, cnt_s, tsem.at[2]),
        pltpu.make_async_copy(nb_hbm, nb_v, tsem.at[3]),
        pltpu.make_async_copy(gain_hbm, gain_v, tsem.at[4]),
        pltpu.make_async_copy(bias_hbm, bias_v, tsem.at[5]),
    ]
    for cp in tables + loads + rest:
        cp.start()
    for cp in tables:
        cp.wait()

    hot = (lax.broadcasted_iota(jnp.int32, (HOLD, B), 0) == own_v[...]).astype(F32)
    upper = (
        lax.broadcasted_iota(jnp.int32, (B, B), 0) <= lax.broadcasted_iota(jnp.int32, (B, B), 1)
    ).astype(BF16)
    order = jnp.dot(hot.astype(BF16), upper, preferred_element_type=F32)
    cnt = cnt_v[...].astype(F32)
    blk = lax.broadcasted_iota(jnp.int32, (HOLD, B), 1).astype(F32)
    lane = lax.broadcasted_iota(jnp.int32, (HOLD, 128), 1)
    tab = jnp.zeros((HOLD, 128), F32)
    for c in range(CAP):
        sel = jnp.where(order == float(c + 1), hot, 0.0)
        tab = jnp.where(lane == c, jnp.sum(sel * blk, axis=1, keepdims=True), tab)
        tab = jnp.where(lane == 16 + c, jnp.sum(sel * cnt, axis=1, keepdims=True), tab)
    tab_v[...] = tab.astype(jnp.int32)
    tab_copy = pltpu.make_async_copy(tab_v, tab_s, lsem.at[CHUNKS + 5])
    tab_copy.start()

    wide[...] = jnp.zeros_like(wide)
    for q in range(2 * CAP):
        wide[q : q + 1, 0:HOLD] = nb_v[q]
    note = jnp.where(lane < 16, wide[...].T[0:HOLD, :], tab_v[...])
    for j in range(HOLD):
        nbs[j] = note[j : j + 1, :]

    row = lax.broadcasted_iota(jnp.int32, (R, D), 0)
    for k in range(CHUNKS):
        loads[k].wait()

        def stat(i, carry):
            for j in range(2):
                b = k * per + i * 2 + j
                x = jnp.where(row < cnt_s[b], facts[b].astype(F32), 0.0)
                bs[pl.ds(b, 1), :] = jnp.sum(x, axis=0, keepdims=True)
                bq[pl.ds(b, 1), :] = jnp.sum(x * x, axis=0, keepdims=True)
            return carry

        lax.fori_loop(0, per // 2, stat, 0)
    sums = jnp.dot(hot, bs[...], preferred_element_type=F32, precision=lax.Precision.HIGHEST)
    squares = jnp.dot(hot, bq[...], preferred_element_type=F32, precision=lax.Precision.HIGHEST)
    live = jnp.broadcast_to(jnp.sum(hot * cnt, axis=1, keepdims=True), (HOLD, 128))
    st[...] = jnp.zeros_like(st)
    for h in range(HOLD):
        base = 3 * (h % 2)
        st[h // 2, base : base + 1, :] = sums[h : h + 1, :]
        st[h // 2, base + 1 : base + 2, :] = squares[h : h + 1, :]
        st[h // 2, base + 2 : base + 3, :] = live[h : h + 1, :]

    tab_copy.wait()
    for d in range(HOLD):
        p = peer(s, d // 4, d % 4)
        x = facts[jnp.clip(tab_s[p, CAP - 1], 0, B - 1)]
        if d:
            xs[p] = x
        else:
            ex[s] = x

    pl.semaphore_wait(bar, TM - 1 + HOLD - 1)

    for i in range(1, TM):
        p = lax.rem(t + i, TM)
        pltpu.make_async_remote_copy(
                src_ref=st.at[p], dst_ref=r1.at[t], send_sem=s1.at[0], recv_sem=q1.at[0],
                device_id={"tm": p}, device_id_type=MESH,
        ).start()
    for d in range(1, HOLD):
        p = peer(s, d // 4, d % 4)
        pltpu.make_async_remote_copy(
                src_ref=nbs.at[p], dst_ref=rnb.at[s], send_sem=sn.at[0], recv_sem=qn.at[0],
                device_id={"hash": p}, device_id_type=MESH,
        ).start()
    for d in range(1, HOLD):
        p = peer(s, d // 4, d % 4)
        pltpu.make_async_remote_copy(
                src_ref=xs.at[p], dst_ref=ex.at[s], send_sem=sx.at[0], recv_sem=qx.at[0],
                device_id={"hash": p}, device_id_type=MESH,
        ).start()
    rnb[s] = nbs[s]
    r1[t] = st[t]
    first.wait_recv()
    r2[s] = jnp.sum(r1[...], axis=0)
    for d in range(1, HOLD):
        p = peer(s, d // 4, d % 4)
        pltpu.make_async_remote_copy(
                src_ref=r2.at[s], dst_ref=r2.at[s], send_sem=s2.at[0], recv_sem=q2.at[0],
                device_id={"hash": p}, device_id_type=MESH,
        ).start()
    asks.wait_recv()
    for h in range(HOLD):
        nbt_v[h : h + 1, :] = rnb[h]
    nb_copy = pltpu.make_async_copy(nbt_v, nb_s, lsem.at[CHUNKS + 6])
    nb_copy.start()
    for cp in rest:
        cp.wait()
    nb_copy.wait()

    def agg_of(p, c):
        e = ent[nb_s[p, 2 * c]].astype(F32) + ent[nb_s[p, 2 * c + 1]].astype(F32)
        return (e * 0.5).astype(BF16)

    for d in range(HOLD):
        p = peer(s, d // 4, d % 4)
        if d:
            ags[p] = agg_of(p, CAP - 1)
            pltpu.make_async_remote_copy(
                    src_ref=ags.at[p], dst_ref=ea.at[s], send_sem=sa.at[0], recv_sem=qa.at[0],
                    device_id={"hash": p}, device_id_type=MESH,
            ).start()
        else:
            ea[s] = agg_of(p, CAP - 1)
    second.wait_recv()
    fin[t] = jnp.sum(r2[...], axis=0)
    for i in range(1, TM):
        p = lax.rem(t + i, TM)
        pltpu.make_async_remote_copy(
                src_ref=fin.at[t], dst_ref=fin.at[t], send_sem=s3.at[0], recv_sem=q3.at[0],
                device_id={"tm": p}, device_id_type=MESH,
        ).start()
    third.wait_recv()
    for h in range(HOLD):
        base = 3 * (h % 2)
        n = fin[h // 2, base + 2 : base + 3, :]
        mean = fin[h // 2, base : base + 1, :] / n
        var = fin[h // 2, base + 1 : base + 2, :] / n - mean * mean
        mean_v[h : h + 1, :] = mean
        scale_v[h : h + 1, :] = lax.rsqrt(var + EPS) * gain_v[...]

    def copy_of(dz, dx, c):
        k = (dz * 4 + dx) * CAP + c
        return pltpu.make_async_remote_copy(
            src_ref=send.at[k], dst_ref=o_ref.at[s * CAP + c], send_sem=ss.at[0], recv_sem=qs.at[0],
            device_id={"hash": peer(s, dz, dx)}, device_id_type=MESH,
        )

    def own_copy(c):
        return pltpu.make_async_copy(send.at[c], o_ref.at[s * CAP + c], lsem.at[CHUNKS + 7])

    def norm_of(x, p):
        x = (x.astype(F32) - mean_v[pl.ds(p, 1), :]) * scale_v[pl.ds(p, 1), :]
        return x.astype(BF16)

    def layers():
        h1 = jnp.dot(in1[...], w1[...], preferred_element_type=F32) + bias_v[...]
        h1 = jnp.maximum(h1, 0.0).astype(BF16)
        h2 = jnp.dot(h1, wmid[...], preferred_element_type=F32)
        h2 = jnp.maximum(h2, 0.0).astype(BF16)
        return jnp.dot(h2, wout[...], preferred_element_type=F32)

    def step(n, carry):
        c, dz = lax.div(n, 4), lax.rem(n, 4)
        for dx in range(4):
            p = peer(s, dz, dx)
            in1[dx * R : (dx + 1) * R, 0:D] = norm_of(facts[jnp.clip(tab_s[p, c], 0, B - 1)], p)
            in1[dx * R : (dx + 1) * R, D : 2 * D] = agg_of(p, c)
        out = layers()
        for dx in range(4):
            p = peer(s, dz, dx)
            y = jnp.where(row < tab_s[p, 16 + c], out[dx * R : (dx + 1) * R, :], 0.0)
            send[(dz * 4 + dx) * CAP + c] = y.astype(BF16)
            if dx:
                copy_of(dz, dx, c).start()
            else:

                @pl.when(dz > 0)
                def _():
                    copy_of(dz, 0, c).start()

                @pl.when(dz == 0)
                def _():
                    own_copy(c).start()

        return carry

    lax.fori_loop(0, 4 * (CAP - 1), step, 0)

    early_x.wait_recv()
    early_a.wait_recv()

    def late_copy(k):
        return pltpu.make_async_copy(ea.at[k], o_ref.at[k * CAP + CAP - 1], lsem.at[CHUNKS + 8])

    def late(n, carry):
        for i in range(4):
            k = n * 4 + i
            in1[i * R : (i + 1) * R, 0:D] = norm_of(ex[k], s)
            in1[i * R : (i + 1) * R, D : 2 * D] = ea[k]
        out = layers()
        for i in range(4):
            k = n * 4 + i
            y = jnp.where(row < nb_s[k, 16 + CAP - 1], out[i * R : (i + 1) * R, :], 0.0)
            ea[k] = y.astype(BF16)
            late_copy(k).start()
        return carry

    lax.fori_loop(0, HOLD // 4, late, 0)

    for cp in (first, asks, second, third, early_x, early_a, rows_out):
        cp.wait_send()
    pltpu.make_async_copy(send.at[pl.ds(0, CAP - 1)], o_ref.at[pl.ds(0, CAP - 1)], lsem.at[CHUNKS + 7]).wait()
    pltpu.make_async_copy(ea, o_ref.at[pl.ds(0, HOLD)], lsem.at[CHUNKS + 8]).wait()
    rows_out.wait_recv()


def body(fact_blocks, owners, row_counts, neighbours, entities, col_gain, w_self, w_nbr, mlp_bias, w_mid, w_out):
    hbm = pl.BlockSpec(memory_space=pl.ANY)
    dma = pltpu.SemaphoreType.DMA
    out = pl.pallas_call(
        kernel,
        out_shape=jax.ShapeDtypeStruct((HOLD * CAP, R, D), BF16),
        in_specs=[hbm] * 12,
        out_specs=hbm,
        scratch_shapes=[
            pltpu.VMEM((1, B), jnp.int32),
            pltpu.VMEM((1, B), jnp.int32),
            pltpu.SMEM((B,), jnp.int32),
            pltpu.VMEM((2 * CAP, 1, HOLD), jnp.int32),
            pltpu.VMEM((1, D), F32),
            pltpu.VMEM((1, HID), F32),
            pltpu.VMEM((B, R, D), BF16),
            pltpu.VMEM((64, R, D), BF16),
            pltpu.VMEM((2 * D, HID), BF16),
            pltpu.VMEM((HID, HID), BF16),
            pltpu.VMEM((HID, D), BF16),
            pltpu.VMEM((B, D), F32),
            pltpu.VMEM((B, D), F32),
            pltpu.VMEM((TM, 8, 128), F32),
            pltpu.VMEM((TM, 8, 128), F32),
            pltpu.VMEM((HOLD, 8, 128), F32),
            pltpu.VMEM((TM, 8, 128), F32),
            pltpu.VMEM((HOLD, 1, 128), jnp.int32),
            pltpu.VMEM((HOLD, 1, 128), jnp.int32),
            pltpu.VMEM((128, 128), jnp.int32),
            pltpu.VMEM((HOLD, 128), jnp.int32),
            pltpu.VMEM((HOLD, 128), jnp.int32),
            pltpu.SMEM((HOLD, 128), jnp.int32),
            pltpu.SMEM((HOLD, 128), jnp.int32),
            pltpu.VMEM((HOLD, D), F32),
            pltpu.VMEM((HOLD, D), F32),
            pltpu.VMEM((4 * R, 2 * D), BF16),
            pltpu.VMEM((HOLD * CAP, R, D), BF16),
            pltpu.VMEM((HOLD, R, D), BF16),
            pltpu.VMEM((HOLD, R, D), BF16),
            pltpu.VMEM((HOLD, R, D), BF16),
            pltpu.VMEM((HOLD, R, D), BF16),
            dma((CHUNKS + 9,)),
            *[dma((1,))] * 14,
            dma((6,)),
        ],
        compiler_params=pltpu.CompilerParams(
            collective_id=0, has_side_effects=True, vmem_limit_bytes=60 << 20
        ),
        cost_estimate=pl.CostEstimate(flops=12 * 10**9, bytes_accessed=10 * 2**20, transcendentals=0),
    )(
        fact_blocks,
        owners.reshape(1, B),
        row_counts.reshape(1, B),
        row_counts,
        neighbours.transpose(2, 0, 1),
        entities,
        col_gain.reshape(1, D),
        w_self,
        w_nbr,
        mlp_bias.reshape(1, HID),
        w_mid,
        w_out,
    )
    return out[None]


def solution(mesh):
    return jax.shard_map(
        body,
        mesh=mesh,
        in_specs=(
            P(("tm", "hash"), None, None),
            P(("tm", "hash")),
            P(("tm", "hash")),
            P(("tm", "hash"), None, None),
            P("hash", None, None),
            P(),
            P(),
            P(),
            P(),
            P(),
            P(),
        ),
        out_specs=P(("tm", "hash"), None, None, None),
        check_vma=False,
    )
```

```python
import functools

import jax
import jax.numpy as jnp
from jax import lax
from jax.experimental import pallas as pl
from jax.experimental.pallas import tpu as pltpu
from jax.sharding import PartitionSpec as P

MESH = pl.DeviceIdType.MESH
HOLD = 16
TM = 8
CAP = 6
B = 48
R = 128
D = 128
HID = 512
EPS = 1e-05
CHUNKS = 4
PIECES = 8
F32 = jnp.float32
BF16 = jnp.bfloat16


def peer(s, dz, dx):
    return lax.rem(lax.div(s, 4) + dz, 4) * 4 + lax.rem(lax.rem(s, 4) + dx, 4)


def kernel(
    fact_hbm, own_hbm, cnt_hbm, cnt1_hbm, nb_hbm, ent_hbm, gain_hbm, wself_hbm, wnbr_hbm, bias_hbm, wmid_hbm, wout_hbm,
    o_ref,
    own_v, cnt_v, cnt_s, nb_v, gain_v, bias_v, facts, ent, w1, wmid, wout, bs, bq, st, r1, r2, fin, nbs, rnb, wide, tab_v, nbt_v, tab_s, nb_s, mean_v, scale_v,
    in1, send, xs, ags, ex, ea, lsem, s1, q1, s2, q2, s3, q3, sn, qn, sx, qx, sa, qa, ss, qs, tsem,
):
    t = lax.axis_index("tm")
    s = lax.axis_index("hash")

    bar = pltpu.get_barrier_semaphore()
    for i in range(1, TM):
        pl.semaphore_signal(bar, inc=1, device_id={"tm": lax.rem(t + i, TM)}, device_id_type=MESH)
    for d in range(1, HOLD):
        pl.semaphore_signal(bar, inc=1, device_id={"hash": peer(s, d // 4, d % 4)}, device_id_type=MESH)

    def group(src, dst, n, send_sem, recv_sem):
        return pltpu.make_async_remote_copy(
            src_ref=src.at[pl.ds(0, n)], dst_ref=dst.at[pl.ds(0, n)], send_sem=send_sem.at[0],
            recv_sem=recv_sem.at[0], device_id={"hash": peer(s, 0, 1)}, device_id_type=MESH,
        )

    first = group(st, r1, TM - 1, s1, q1)
    asks = group(nbs, rnb, HOLD - 1, sn, qn)
    second = group(r2, r2, HOLD - 1, s2, q2)
    third = group(fin, fin, TM - 1, s3, q3)
    early_x = group(xs, ex, HOLD - 1, sx, qx)
    early_a = group(ags, ea, HOLD - 1, sa, qa)
    rows_out = group(send, o_ref, (HOLD - 1) * (CAP - 1), ss, qs)

    per = B // CHUNKS
    loads = [
        pltpu.make_async_copy(fact_hbm.at[pl.ds(k * per, per)], facts.at[pl.ds(k * per, per)], lsem.at[k])
        for k in range(CHUNKS)
    ]
    rest = [
        pltpu.make_async_copy(wself_hbm, w1.at[pl.ds(0, D)], lsem.at[CHUNKS]),
        pltpu.make_async_copy(wnbr_hbm, w1.at[pl.ds(D, D)], lsem.at[CHUNKS + 1]),
        pltpu.make_async_copy(wmid_hbm, wmid, lsem.at[CHUNKS + 2]),
        pltpu.make_async_copy(wout_hbm, wout, lsem.at[CHUNKS + 3]),
        pltpu.make_async_copy(ent_hbm, ent, lsem.at[CHUNKS + 4]),
    ]
    tables = [
        pltpu.make_async_copy(own_hbm, own_v, tsem.at[0]),
        pltpu.make_async_copy(cnt_hbm, cnt_v, tsem.at[1]),
        pltpu.make_async_copy(cnt1_hbm, cnt_s, tsem.at[2]),
        pltpu.make_async_copy(nb_hbm, nb_v, tsem.at[3]),
        pltpu.make_async_copy(gain_hbm, gain_v, tsem.at[4]),
        pltpu.make_async_copy(bias_hbm, bias_v, tsem.at[5]),
    ]
    for cp in tables + loads + rest:
        cp.start()
    for cp in tables:
        cp.wait()

    hot = (lax.broadcasted_iota(jnp.int32, (HOLD, B), 0) == own_v[...]).astype(F32)
    upper = (
        lax.broadcasted_iota(jnp.int32, (B, B), 0) <= lax.broadcasted_iota(jnp.int32, (B, B), 1)
    ).astype(BF16)
    order = jnp.dot(hot.astype(BF16), upper, preferred_element_type=F32)
    cnt = cnt_v[...].astype(F32)
    blk = lax.broadcasted_iota(jnp.int32, (HOLD, B), 1).astype(F32)
    lane = lax.broadcasted_iota(jnp.int32, (HOLD, 128), 1)
    tab = jnp.zeros((HOLD, 128), F32)
    for c in range(CAP):
        sel = jnp.where(order == float(c + 1), hot, 0.0)
        tab = jnp.where(lane == c, jnp.sum(sel * blk, axis=1, keepdims=True), tab)
        tab = jnp.where(lane == 16 + c, jnp.sum(sel * cnt, axis=1, keepdims=True), tab)
    tab_v[...] = tab.astype(jnp.int32)
    tab_copy = pltpu.make_async_copy(tab_v, tab_s, lsem.at[CHUNKS + 5])
    tab_copy.start()

    wide[...] = jnp.zeros_like(wide)
    for q in range(2 * CAP):
        wide[q : q + 1, 0:HOLD] = nb_v[q]
    note = jnp.where(lane < 16, wide[...].T[0:HOLD, :], tab_v[...])
    for j in range(HOLD):
        nbs[j] = note[j : j + 1, :]

    row = lax.broadcasted_iota(jnp.int32, (R, D), 0)
    for k in range(CHUNKS):
        loads[k].wait()

        def stat(i, carry):
            for j in range(2):
                b = k * per + i * 2 + j
                x = jnp.where(row < cnt_s[b], facts[b].astype(F32), 0.0)
                bs[pl.ds(b, 1), :] = jnp.sum(x, axis=0, keepdims=True)
                bq[pl.ds(b, 1), :] = jnp.sum(x * x, axis=0, keepdims=True)
            return carry

        lax.fori_loop(0, per // 2, stat, 0)
    sums = jnp.dot(hot, bs[...], preferred_element_type=F32, precision=lax.Precision.HIGHEST)
    squares = jnp.dot(hot, bq[...], preferred_element_type=F32, precision=lax.Precision.HIGHEST)
    live = jnp.broadcast_to(jnp.sum(hot * cnt, axis=1, keepdims=True), (HOLD, 128))
    st[...] = jnp.zeros_like(st)
    for h in range(HOLD):
        base = 3 * (h % 2)
        st[h // 2, base : base + 1, :] = sums[h : h + 1, :]
        st[h // 2, base + 1 : base + 2, :] = squares[h : h + 1, :]
        st[h // 2, base + 2 : base + 3, :] = live[h : h + 1, :]

    tab_copy.wait()
    for d in range(HOLD):
        p = peer(s, d // 4, d % 4)
        x = facts[jnp.clip(tab_s[p, CAP - 1], 0, B - 1)]
        if d:
            xs[p] = x
        else:
            ex[s] = x

    pl.semaphore_wait(bar, TM - 1 + HOLD - 1)

    for i in range(1, TM):
        p = lax.rem(t + i, TM)
        pltpu.make_async_remote_copy(
                src_ref=st.at[p], dst_ref=r1.at[t], send_sem=s1.at[0], recv_sem=q1.at[0],
                device_id={"tm": p}, device_id_type=MESH,
        ).start()
    for d in range(1, HOLD):
        p = peer(s, d // 4, d % 4)
        pltpu.make_async_remote_copy(
                src_ref=nbs.at[p], dst_ref=rnb.at[s], send_sem=sn.at[0], recv_sem=qn.at[0],
                device_id={"hash": p}, device_id_type=MESH,
        ).start()
    for d in range(1, HOLD):
        p = peer(s, d // 4, d % 4)
        pltpu.make_async_remote_copy(
                src_ref=xs.at[p], dst_ref=ex.at[s], send_sem=sx.at[0], recv_sem=qx.at[0],
                device_id={"hash": p}, device_id_type=MESH,
        ).start()
    rnb[s] = nbs[s]
    r1[t] = st[t]
    first.wait_recv()
    r2[s] = jnp.sum(r1[...], axis=0)
    for d in range(1, HOLD):
        p = peer(s, d // 4, d % 4)
        pltpu.make_async_remote_copy(
                src_ref=r2.at[s], dst_ref=r2.at[s], send_sem=s2.at[0], recv_sem=q2.at[0],
                device_id={"hash": p}, device_id_type=MESH,
        ).start()
    asks.wait_recv()
    for h in range(HOLD):
        nbt_v[h : h + 1, :] = rnb[h]
    nb_copy = pltpu.make_async_copy(nbt_v, nb_s, lsem.at[CHUNKS + 6])
    nb_copy.start()
    for cp in rest:
        cp.wait()
    nb_copy.wait()

    def agg_of(p, c):
        e = ent[nb_s[p, 2 * c]].astype(F32) + ent[nb_s[p, 2 * c + 1]].astype(F32)
        return (e * 0.5).astype(BF16)

    for d in range(HOLD):
        p = peer(s, d // 4, d % 4)
        if d:
            ags[p] = agg_of(p, CAP - 1)
            pltpu.make_async_remote_copy(
                    src_ref=ags.at[p], dst_ref=ea.at[s], send_sem=sa.at[0], recv_sem=qa.at[0],
                    device_id={"hash": p}, device_id_type=MESH,
            ).start()
        else:
            ea[s] = agg_of(p, CAP - 1)
    second.wait_recv()
    fin[t] = jnp.sum(r2[...], axis=0)
    for i in range(1, TM):
        p = lax.rem(t + i, TM)
        pltpu.make_async_remote_copy(
                src_ref=fin.at[t], dst_ref=fin.at[t], send_sem=s3.at[0], recv_sem=q3.at[0],
                device_id={"tm": p}, device_id_type=MESH,
        ).start()
    third.wait_recv()
    for h in range(HOLD):
        base = 3 * (h % 2)
        n = fin[h // 2, base + 2 : base + 3, :]
        mean = fin[h // 2, base : base + 1, :] / n
        var = fin[h // 2, base + 1 : base + 2, :] / n - mean * mean
        mean_v[h : h + 1, :] = mean
        scale_v[h : h + 1, :] = lax.rsqrt(var + EPS) * gain_v[...]

    def copy_of(dz, dx, c):
        k = (dz * 4 + dx) * CAP + c
        return pltpu.make_async_remote_copy(
            src_ref=send.at[k], dst_ref=o_ref.at[s * CAP + c], send_sem=ss.at[0], recv_sem=qs.at[0],
            device_id={"hash": peer(s, dz, dx)}, device_id_type=MESH,
        )

    def own_copy(c):
        return pltpu.make_async_copy(send.at[c], o_ref.at[s * CAP + c], lsem.at[CHUNKS + 7])

    def norm_of(x, p):
        x = (x.astype(F32) - mean_v[pl.ds(p, 1), :]) * scale_v[pl.ds(p, 1), :]
        return x.astype(BF16)

    def layers():
        h1 = jnp.dot(in1[...], w1[...], preferred_element_type=F32) + bias_v[...]
        h1 = jnp.maximum(h1, 0.0).astype(BF16)
        h2 = jnp.dot(h1, wmid[...], preferred_element_type=F32)
        h2 = jnp.maximum(h2, 0.0).astype(BF16)
        return jnp.dot(h2, wout[...], preferred_element_type=F32)

    def step(n, carry):
        c, dz = lax.div(n, 4), lax.rem(n, 4)
        for dx in range(4):
            p = peer(s, dz, dx)
            in1[dx * R : (dx + 1) * R, 0:D] = norm_of(facts[jnp.clip(tab_s[p, c], 0, B - 1)], p)
            in1[dx * R : (dx + 1) * R, D : 2 * D] = agg_of(p, c)
        out = layers()
        for dx in range(4):
            p = peer(s, dz, dx)
            y = jnp.where(row < tab_s[p, 16 + c], out[dx * R : (dx + 1) * R, :], 0.0)
            send[(dz * 4 + dx) * CAP + c] = y.astype(BF16)
            if dx:
                copy_of(dz, dx, c).start()
            else:

                @pl.when(dz > 0)
                def _():
                    copy_of(dz, 0, c).start()

                @pl.when(dz == 0)
                def _():
                    own_copy(c).start()

        return carry

    lax.fori_loop(0, 4 * (CAP - 1), step, 0)

    early_x.wait_recv()
    early_a.wait_recv()

    def late_copy(k):
        return pltpu.make_async_copy(ea.at[k], o_ref.at[k * CAP + CAP - 1], lsem.at[CHUNKS + 8])

    def late(n, carry):
        for i in range(4):
            k = n * 4 + i
            in1[i * R : (i + 1) * R, 0:D] = norm_of(ex[k], s)
            in1[i * R : (i + 1) * R, D : 2 * D] = ea[k]
        out = layers()
        for i in range(4):
            k = n * 4 + i
            y = jnp.where(row < nb_s[k, 16 + CAP - 1], out[i * R : (i + 1) * R, :], 0.0)
            ea[k] = y.astype(BF16)
            late_copy(k).start()
        return carry

    lax.fori_loop(0, HOLD // 4, late, 0)

    for cp in (first, asks, second, third, early_x, early_a, rows_out):
        cp.wait_send()
    pltpu.make_async_copy(send.at[pl.ds(0, CAP - 1)], o_ref.at[pl.ds(0, CAP - 1)], lsem.at[CHUNKS + 7]).wait()
    pltpu.make_async_copy(ea, o_ref.at[pl.ds(0, HOLD)], lsem.at[CHUNKS + 8]).wait()
    rows_out.wait_recv()


def place(x_ref, o_ref, buf, rsem, wsem):
    per = HOLD * CAP // PIECES
    reads, writes = [], []
    for k in range(PIECES):
        part = pl.ds(k * per, per)
        reads.append(pltpu.make_async_copy(x_ref.at[part], buf.at[part], rsem.at[k]))
        writes.append(pltpu.make_async_copy(buf.at[part], o_ref.at[0, part], wsem.at[k]))
        reads[-1].start()
    for read, write in zip(reads, writes):
        read.wait()
        write.start()
    for write in writes:
        write.wait()


def body(fact_blocks, owners, row_counts, neighbours, entities, col_gain, w_self, w_nbr, mlp_bias, w_mid, w_out):
    hbm = pl.BlockSpec(memory_space=pl.ANY)
    dma = pltpu.SemaphoreType.DMA
    out = pl.pallas_call(
        kernel,
        out_shape=jax.ShapeDtypeStruct((HOLD * CAP, R, D), BF16),
        in_specs=[hbm] * 12,
        out_specs=hbm,
        scratch_shapes=[
            pltpu.VMEM((1, B), jnp.int32),
            pltpu.VMEM((1, B), jnp.int32),
            pltpu.SMEM((B,), jnp.int32),
            pltpu.VMEM((2 * CAP, 1, HOLD), jnp.int32),
            pltpu.VMEM((1, D), F32),
            pltpu.VMEM((1, HID), F32),
            pltpu.VMEM((B, R, D), BF16),
            pltpu.VMEM((64, R, D), BF16),
            pltpu.VMEM((2 * D, HID), BF16),
            pltpu.VMEM((HID, HID), BF16),
            pltpu.VMEM((HID, D), BF16),
            pltpu.VMEM((B, D), F32),
            pltpu.VMEM((B, D), F32),
            pltpu.VMEM((TM, 8, 128), F32),
            pltpu.VMEM((TM, 8, 128), F32),
            pltpu.VMEM((HOLD, 8, 128), F32),
            pltpu.VMEM((TM, 8, 128), F32),
            pltpu.VMEM((HOLD, 1, 128), jnp.int32),
            pltpu.VMEM((HOLD, 1, 128), jnp.int32),
            pltpu.VMEM((128, 128), jnp.int32),
            pltpu.VMEM((HOLD, 128), jnp.int32),
            pltpu.VMEM((HOLD, 128), jnp.int32),
            pltpu.SMEM((HOLD, 128), jnp.int32),
            pltpu.SMEM((HOLD, 128), jnp.int32),
            pltpu.VMEM((HOLD, D), F32),
            pltpu.VMEM((HOLD, D), F32),
            pltpu.VMEM((4 * R, 2 * D), BF16),
            pltpu.VMEM((HOLD * CAP, R, D), BF16),
            pltpu.VMEM((HOLD, R, D), BF16),
            pltpu.VMEM((HOLD, R, D), BF16),
            pltpu.VMEM((HOLD, R, D), BF16),
            pltpu.VMEM((HOLD, R, D), BF16),
            dma((CHUNKS + 9,)),
            *[dma((1,))] * 14,
            dma((6,)),
        ],
        compiler_params=pltpu.CompilerParams(
            collective_id=0, has_side_effects=True, vmem_limit_bytes=60 << 20
        ),
        cost_estimate=pl.CostEstimate(flops=12 * 10**9, bytes_accessed=10 * 2**20, transcendentals=0),
    )(
        fact_blocks,
        owners.reshape(1, B),
        row_counts.reshape(1, B),
        row_counts,
        neighbours.transpose(2, 0, 1),
        entities,
        col_gain.reshape(1, D),
        w_self,
        w_nbr,
        mlp_bias.reshape(1, HID),
        w_mid,
        w_out,
    )
    return pl.pallas_call(
        place,
        out_shape=jax.ShapeDtypeStruct((1, HOLD * CAP, R, D), BF16),
        in_specs=[hbm],
        out_specs=hbm,
        scratch_shapes=[pltpu.VMEM((HOLD * CAP, R, D), BF16), dma((PIECES,)), dma((PIECES,))],
        compiler_params=pltpu.CompilerParams(vmem_limit_bytes=60 << 20),
    )(out)


def solution(mesh):
    return jax.shard_map(
        body,
        mesh=mesh,
        in_specs=(
            P(("tm", "hash"), None, None),
            P(("tm", "hash")),
            P(("tm", "hash")),
            P(("tm", "hash"), None, None),
            P("hash", None, None),
            P(),
            P(),
            P(),
            P(),
            P(),
            P(),
        ),
        out_specs=P(("tm", "hash"), None, None, None),
        check_vma=False,
    )
```

```python
import functools

import jax
import jax.numpy as jnp
from jax import lax
from jax.experimental import pallas as pl
from jax.experimental.pallas import tpu as pltpu
from jax.sharding import PartitionSpec as P

MESH = pl.DeviceIdType.MESH
HOLD = 16
TM = 8
CAP = 6
B = 48
R = 128
D = 128
HID = 512
EPS = 1e-05
CHUNKS = 4
PIECES = 8
F32 = jnp.float32
BF16 = jnp.bfloat16


def peer(s, dz, dx):
    return lax.rem(lax.div(s, 4) + dz, 4) * 4 + lax.rem(lax.rem(s, 4) + dx, 4)


def kernel(
    fact_hbm, own_hbm, cnt_hbm, cnt1_hbm, nb_hbm, ent_hbm, gain_hbm, wself_hbm, wnbr_hbm, bias_hbm, wmid_hbm, wout_hbm,
    o_ref,
    own_v, cnt_v, cnt_s, nb_v, gain_v, bias_v, facts, ent, w1, wmid, wout, bs, bq, st, r1, r2, fin, nbs, rnb, wide, tab_v, nbt_v, tab_s, nb_s, mean_v, scale_v,
    in1, send, xs, ags, ex, ea, lsem, s1, q1, s2, q2, s3, q3, sn, qn, sx, qx, sa, qa, ss, qs, tsem,
):
    t = lax.axis_index("tm")
    s = lax.axis_index("hash")

    zs = [lax.rem(lax.div(s, 4) + d, 4) * 4 for d in range(4)]
    xc = [lax.rem(lax.rem(s, 4) + d, 4) for d in range(4)]
    near = [s] + [zs[d // 4] + xc[d % 4] for d in range(1, HOLD)]
    times = [t] + [lax.rem(t + i, TM) for i in range(1, TM)]

    def group(src, dst, n, send_sem, recv_sem):
        return pltpu.make_async_remote_copy(
            src_ref=src.at[pl.ds(0, n)], dst_ref=dst.at[pl.ds(0, n)], send_sem=send_sem.at[0],
            recv_sem=recv_sem.at[0], device_id={"hash": peer(s, 0, 1)}, device_id_type=MESH,
        )

    first = group(st, r1, TM - 1, s1, q1)
    asks = group(nbs, rnb, HOLD - 1, sn, qn)
    second = group(r2, r2, HOLD - 1, s2, q2)
    third = group(fin, fin, TM - 1, s3, q3)
    early_x = group(xs, ex, HOLD - 1, sx, qx)
    early_a = group(ags, ea, HOLD - 1, sa, qa)
    rows_out = group(send, o_ref, (HOLD - 1) * (CAP - 1), ss, qs)

    per = B // CHUNKS
    loads = [
        pltpu.make_async_copy(fact_hbm.at[pl.ds(k * per, per)], facts.at[pl.ds(k * per, per)], lsem.at[k])
        for k in range(CHUNKS)
    ]
    rest = [
        pltpu.make_async_copy(wself_hbm, w1.at[pl.ds(0, D)], lsem.at[CHUNKS]),
        pltpu.make_async_copy(wnbr_hbm, w1.at[pl.ds(D, D)], lsem.at[CHUNKS + 1]),
        pltpu.make_async_copy(wmid_hbm, wmid, lsem.at[CHUNKS + 2]),
        pltpu.make_async_copy(wout_hbm, wout, lsem.at[CHUNKS + 3]),
        pltpu.make_async_copy(ent_hbm, ent, lsem.at[CHUNKS + 4]),
    ]
    tables = [
        pltpu.make_async_copy(own_hbm, own_v, tsem.at[0]),
        pltpu.make_async_copy(cnt_hbm, cnt_v, tsem.at[1]),
        pltpu.make_async_copy(cnt1_hbm, cnt_s, tsem.at[2]),
        pltpu.make_async_copy(nb_hbm, nb_v, tsem.at[3]),
        pltpu.make_async_copy(gain_hbm, gain_v, tsem.at[4]),
        pltpu.make_async_copy(bias_hbm, bias_v, tsem.at[5]),
    ]
    for cp in tables + loads:
        cp.start()

    bar = pltpu.get_barrier_semaphore()
    for i in range(1, TM):
        pl.semaphore_signal(bar, inc=1, device_id={"tm": times[i]}, device_id_type=MESH)
    for d in range(1, HOLD):
        pl.semaphore_signal(bar, inc=1, device_id={"hash": near[d]}, device_id_type=MESH)

    for cp in rest:
        cp.start()
    for cp in tables:
        cp.wait()

    hot = (lax.broadcasted_iota(jnp.int32, (HOLD, B), 0) == own_v[...]).astype(F32)
    upper = (
        lax.broadcasted_iota(jnp.int32, (B, B), 0) <= lax.broadcasted_iota(jnp.int32, (B, B), 1)
    ).astype(BF16)
    order = jnp.dot(hot.astype(BF16), upper, preferred_element_type=F32)
    cnt = cnt_v[...].astype(F32)
    blk = lax.broadcasted_iota(jnp.int32, (HOLD, B), 1).astype(F32)
    lane = lax.broadcasted_iota(jnp.int32, (HOLD, 128), 1)
    tab = jnp.zeros((HOLD, 128), F32)
    for c in range(CAP):
        sel = jnp.where(order == float(c + 1), hot, 0.0)
        tab = jnp.where(lane == c, jnp.sum(sel * blk, axis=1, keepdims=True), tab)
        tab = jnp.where(lane == 16 + c, jnp.sum(sel * cnt, axis=1, keepdims=True), tab)
    tab_v[...] = tab.astype(jnp.int32)
    tab_copy = pltpu.make_async_copy(tab_v, tab_s, lsem.at[CHUNKS + 5])
    tab_copy.start()

    wide[...] = jnp.zeros_like(wide)
    for q in range(2 * CAP):
        wide[q : q + 1, 0:HOLD] = nb_v[q]
    note = jnp.where(lane < 16, wide[...].T[0:HOLD, :], tab_v[...])
    for j in range(HOLD):
        nbs[j] = note[j : j + 1, :]

    row = lax.broadcasted_iota(jnp.int32, (R, D), 0)
    for k in range(CHUNKS):
        loads[k].wait()

        def stat(i, carry):
            for j in range(2):
                b = k * per + i * 2 + j
                x = jnp.where(row < cnt_s[b], facts[b].astype(F32), 0.0)
                bs[pl.ds(b, 1), :] = jnp.sum(x, axis=0, keepdims=True)
                bq[pl.ds(b, 1), :] = jnp.sum(x * x, axis=0, keepdims=True)
            return carry

        lax.fori_loop(0, per // 2, stat, 0)
    sums = jnp.dot(hot, bs[...], preferred_element_type=F32, precision=lax.Precision.HIGHEST)
    squares = jnp.dot(hot, bq[...], preferred_element_type=F32, precision=lax.Precision.HIGHEST)
    live = jnp.broadcast_to(jnp.sum(hot * cnt, axis=1, keepdims=True), (HOLD, 128))
    st[...] = jnp.zeros_like(st)
    fin[...] = jnp.zeros_like(fin)
    for h in range(HOLD):
        base = 3 * (h % 2)
        st[h // 2, base : base + 1, :] = sums[h : h + 1, :]
        st[h // 2, base + 1 : base + 2, :] = squares[h : h + 1, :]
        st[h // 2, base + 2 : base + 3, :] = live[h : h + 1, :]

    tab_copy.wait()
    for d in range(HOLD):
        p = near[d]
        x = facts[jnp.clip(tab_s[p, CAP - 1], 0, B - 1)]
        if d:
            xs[p] = x
        else:
            ex[s] = x

    pl.semaphore_wait(bar, TM - 1 + HOLD - 1)

    for i in range(1, TM):
        p = times[i]
        pltpu.make_async_remote_copy(
            src_ref=st.at[p], dst_ref=r1.at[t], send_sem=s1.at[0], recv_sem=q1.at[0],
            device_id={"tm": p}, device_id_type=MESH,
        ).start()
    for d in range(1, HOLD):
        p = near[d]
        pltpu.make_async_remote_copy(
            src_ref=nbs.at[p], dst_ref=rnb.at[s], send_sem=sn.at[0], recv_sem=qn.at[0],
            device_id={"hash": p}, device_id_type=MESH,
        ).start()
    for d in range(1, HOLD):
        p = near[d]
        pltpu.make_async_remote_copy(
            src_ref=xs.at[p], dst_ref=ex.at[s], send_sem=sx.at[0], recv_sem=qx.at[0],
            device_id={"hash": p}, device_id_type=MESH,
        ).start()
    rnb[s] = nbs[s]
    r1[t] = st[t]
    first.wait_recv()
    r2[s] = jnp.sum(r1[...], axis=0)
    for d in range(1, HOLD):
        p = near[d]
        pltpu.make_async_remote_copy(
            src_ref=r2.at[s], dst_ref=r2.at[s], send_sem=s2.at[0], recv_sem=q2.at[0],
            device_id={"hash": p}, device_id_type=MESH,
        ).start()
    asks.wait_recv()
    for h in range(HOLD):
        nbt_v[h : h + 1, :] = rnb[h]
    nb_copy = pltpu.make_async_copy(nbt_v, nb_s, lsem.at[CHUNKS + 6])
    nb_copy.start()
    second.wait_recv()
    total = jnp.sum(r2[...], axis=0)
    for k in range(2):
        mean = total[3 * k : 3 * k + 1, :] / total[3 * k + 2 : 3 * k + 3, :]
        var = total[3 * k + 1 : 3 * k + 2, :] / total[3 * k + 2 : 3 * k + 3, :] - mean * mean
        fin[t, 2 * k : 2 * k + 1, :] = mean
        fin[t, 2 * k + 1 : 2 * k + 2, :] = lax.rsqrt(var + EPS) * gain_v[...]
    for i in range(1, TM):
        p = times[i]
        pltpu.make_async_remote_copy(
            src_ref=fin.at[t], dst_ref=fin.at[t], send_sem=s3.at[0], recv_sem=q3.at[0],
            device_id={"tm": p}, device_id_type=MESH,
        ).start()
    for cp in rest:
        cp.wait()
    nb_copy.wait()

    def agg_of(p, c):
        e = ent[nb_s[p, 2 * c]].astype(F32) + ent[nb_s[p, 2 * c + 1]].astype(F32)
        return (e * 0.5).astype(BF16)

    for d in range(HOLD):
        p = near[d]
        if d:
            ags[p] = agg_of(p, CAP - 1)
            pltpu.make_async_remote_copy(
                    src_ref=ags.at[p], dst_ref=ea.at[s], send_sem=sa.at[0], recv_sem=qa.at[0],
                    device_id={"hash": p}, device_id_type=MESH,
            ).start()
        else:
            ea[s] = agg_of(p, CAP - 1)
    third.wait_recv()
    for h in range(HOLD):
        mean_v[h : h + 1, :] = fin[h // 2, 2 * (h % 2) : 2 * (h % 2) + 1, :]
        scale_v[h : h + 1, :] = fin[h // 2, 2 * (h % 2) + 1 : 2 * (h % 2) + 2, :]

    def copy_of(dz, dx, c):
        k = (dz * 4 + dx) * CAP + c
        return pltpu.make_async_remote_copy(
            src_ref=send.at[k], dst_ref=o_ref.at[s * CAP + c], send_sem=ss.at[0], recv_sem=qs.at[0],
            device_id={"hash": peer(s, dz, dx)}, device_id_type=MESH,
        )

    def own_copy(c):
        return pltpu.make_async_copy(send.at[c], o_ref.at[s * CAP + c], lsem.at[CHUNKS + 7])

    def norm_of(x, p):
        x = (x.astype(F32) - mean_v[pl.ds(p, 1), :]) * scale_v[pl.ds(p, 1), :]
        return x.astype(BF16)

    def layers():
        h1 = jnp.dot(in1[...], w1[...], preferred_element_type=F32) + bias_v[...]
        h1 = jnp.maximum(h1, 0.0).astype(BF16)
        h2 = jnp.dot(h1, wmid[...], preferred_element_type=F32)
        h2 = jnp.maximum(h2, 0.0).astype(BF16)
        return jnp.dot(h2, wout[...], preferred_element_type=F32)

    def step(n, carry):
        c, dz = lax.div(n, 4), lax.rem(n, 4)
        for dx in range(4):
            p = peer(s, dz, dx)
            in1[dx * R : (dx + 1) * R, 0:D] = norm_of(facts[jnp.clip(tab_s[p, c], 0, B - 1)], p)
            in1[dx * R : (dx + 1) * R, D : 2 * D] = agg_of(p, c)
        out = layers()
        for dx in range(4):
            p = peer(s, dz, dx)
            y = jnp.where(row < tab_s[p, 16 + c], out[dx * R : (dx + 1) * R, :], 0.0)
            send[(dz * 4 + dx) * CAP + c] = y.astype(BF16)
            if dx:
                copy_of(dz, dx, c).start()
            else:

                @pl.when(dz > 0)
                def _():
                    copy_of(dz, 0, c).start()

                @pl.when(dz == 0)
                def _():
                    own_copy(c).start()

        return carry

    lax.fori_loop(0, 4 * (CAP - 1), step, 0)

    early_x.wait_recv()
    early_a.wait_recv()

    def late_copy(k):
        return pltpu.make_async_copy(ea.at[k], o_ref.at[k * CAP + CAP - 1], lsem.at[CHUNKS + 8])

    def late(n, carry):
        for i in range(4):
            k = n * 4 + i
            in1[i * R : (i + 1) * R, 0:D] = norm_of(ex[k], s)
            in1[i * R : (i + 1) * R, D : 2 * D] = ea[k]
        out = layers()
        for i in range(4):
            k = n * 4 + i
            y = jnp.where(row < nb_s[k, 16 + CAP - 1], out[i * R : (i + 1) * R, :], 0.0)
            ea[k] = y.astype(BF16)
            late_copy(k).start()
        return carry

    lax.fori_loop(0, HOLD // 4, late, 0)

    for cp in (first, asks, second, third, early_x, early_a, rows_out):
        cp.wait_send()
    pltpu.make_async_copy(send.at[pl.ds(0, CAP - 1)], o_ref.at[pl.ds(0, CAP - 1)], lsem.at[CHUNKS + 7]).wait()
    pltpu.make_async_copy(ea, o_ref.at[pl.ds(0, HOLD)], lsem.at[CHUNKS + 8]).wait()
    rows_out.wait_recv()


def place(x_ref, o_ref, buf, rsem, wsem):
    per = HOLD * CAP // PIECES
    reads, writes = [], []
    for k in range(PIECES):
        part = pl.ds(k * per, per)
        reads.append(pltpu.make_async_copy(x_ref.at[part], buf.at[part], rsem.at[k]))
        writes.append(pltpu.make_async_copy(buf.at[part], o_ref.at[0, part], wsem.at[k]))
        reads[-1].start()
    for read, write in zip(reads, writes):
        read.wait()
        write.start()
    for write in writes:
        write.wait()


def body(fact_blocks, owners, row_counts, neighbours, entities, col_gain, w_self, w_nbr, mlp_bias, w_mid, w_out):
    hbm = pl.BlockSpec(memory_space=pl.ANY)
    dma = pltpu.SemaphoreType.DMA
    out = pl.pallas_call(
        kernel,
        out_shape=jax.ShapeDtypeStruct((HOLD * CAP, R, D), BF16),
        in_specs=[hbm] * 12,
        out_specs=hbm,
        scratch_shapes=[
            pltpu.VMEM((1, B), jnp.int32),
            pltpu.VMEM((1, B), jnp.int32),
            pltpu.SMEM((B,), jnp.int32),
            pltpu.VMEM((2 * CAP, 1, HOLD), jnp.int32),
            pltpu.VMEM((1, D), F32),
            pltpu.VMEM((1, HID), F32),
            pltpu.VMEM((B, R, D), BF16),
            pltpu.VMEM((64, R, D), BF16),
            pltpu.VMEM((2 * D, HID), BF16),
            pltpu.VMEM((HID, HID), BF16),
            pltpu.VMEM((HID, D), BF16),
            pltpu.VMEM((B, D), F32),
            pltpu.VMEM((B, D), F32),
            pltpu.VMEM((TM, 8, 128), F32),
            pltpu.VMEM((TM, 8, 128), F32),
            pltpu.VMEM((HOLD, 8, 128), F32),
            pltpu.VMEM((TM, 8, 128), F32),
            pltpu.VMEM((HOLD, 1, 128), jnp.int32),
            pltpu.VMEM((HOLD, 1, 128), jnp.int32),
            pltpu.VMEM((128, 128), jnp.int32),
            pltpu.VMEM((HOLD, 128), jnp.int32),
            pltpu.VMEM((HOLD, 128), jnp.int32),
            pltpu.SMEM((HOLD, 128), jnp.int32),
            pltpu.SMEM((HOLD, 128), jnp.int32),
            pltpu.VMEM((HOLD, D), F32),
            pltpu.VMEM((HOLD, D), F32),
            pltpu.VMEM((4 * R, 2 * D), BF16),
            pltpu.VMEM((HOLD * CAP, R, D), BF16),
            pltpu.VMEM((HOLD, R, D), BF16),
            pltpu.VMEM((HOLD, R, D), BF16),
            pltpu.VMEM((HOLD, R, D), BF16),
            pltpu.VMEM((HOLD, R, D), BF16),
            dma((CHUNKS + 9,)),
            *[dma((1,))] * 14,
            dma((6,)),
        ],
        compiler_params=pltpu.CompilerParams(
            collective_id=0, has_side_effects=True, vmem_limit_bytes=60 << 20
        ),
        cost_estimate=pl.CostEstimate(flops=12 * 10**9, bytes_accessed=10 * 2**20, transcendentals=0),
    )(
        fact_blocks,
        owners.reshape(1, B),
        row_counts.reshape(1, B),
        row_counts,
        neighbours.transpose(2, 0, 1),
        entities,
        col_gain.reshape(1, D),
        w_self,
        w_nbr,
        mlp_bias.reshape(1, HID),
        w_mid,
        w_out,
    )
    return pl.pallas_call(
        place,
        out_shape=jax.ShapeDtypeStruct((1, HOLD * CAP, R, D), BF16),
        in_specs=[hbm],
        out_specs=hbm,
        scratch_shapes=[pltpu.VMEM((HOLD * CAP, R, D), BF16), dma((PIECES,)), dma((PIECES,))],
        compiler_params=pltpu.CompilerParams(vmem_limit_bytes=60 << 20),
    )(out)


def solution(mesh):
    return jax.shard_map(
        body,
        mesh=mesh,
        in_specs=(
            P(("tm", "hash"), None, None),
            P(("tm", "hash")),
            P(("tm", "hash")),
            P(("tm", "hash"), None, None),
            P("hash", None, None),
            P(),
            P(),
            P(),
            P(),
            P(),
            P(),
        ),
        out_specs=P(("tm", "hash"), None, None, None),
        check_vma=False,
    )
```

```python
import functools

import jax
import jax.numpy as jnp
from jax import lax
from jax.experimental import pallas as pl
from jax.experimental.pallas import tpu as pltpu
from jax.sharding import PartitionSpec as P

MESH = pl.DeviceIdType.MESH
HOLD = 16
TM = 8
CAP = 6
B = 48
R = 128
D = 128
HID = 512
EPS = 1e-05
CHUNKS = 4
PIECES = 8
F32 = jnp.float32
BF16 = jnp.bfloat16


def peer(s, dz, dx):
    return lax.rem(lax.div(s, 4) + dz, 4) * 4 + lax.rem(lax.rem(s, 4) + dx, 4)


def kernel(
    fact_hbm, own_hbm, cnt_hbm, cnt1_hbm, nb_hbm, ent_hbm, gain_hbm, wself_hbm, wnbr_hbm, bias_hbm, wmid_hbm, wout_hbm,
    o_ref,
    own_v, cnt_v, cnt_s, nb_v, gain_v, bias_v, facts, ent, w1, wmid, wout, bs, bq, st, r1, r2, fin, nbs, rnb, wide, tab_v, nbt_v, tab_s, nb_s, mean_v, scale_v,
    in1, send, xs, ags, ex, ea, lsem, s1, q1, s2, q2, s3, q3, sn, qn, sx, qx, sa, qa, ss, qs, tsem,
):
    t = lax.axis_index("tm")
    s = lax.axis_index("hash")

    zs = [lax.rem(lax.div(s, 4) + d, 4) * 4 for d in range(4)]
    xc = [lax.rem(lax.rem(s, 4) + d, 4) for d in range(4)]
    near = [s] + [zs[d // 4] + xc[d % 4] for d in (10, 6, 9, 14, 11, 2, 8, 5, 7, 13, 15, 1, 4, 3, 12)]
    times = [t] + [lax.rem(t + i, TM) for i in range(1, TM)]

    def group(src, dst, n, send_sem, recv_sem):
        return pltpu.make_async_remote_copy(
            src_ref=src.at[pl.ds(0, n)], dst_ref=dst.at[pl.ds(0, n)], send_sem=send_sem.at[0],
            recv_sem=recv_sem.at[0], device_id={"hash": peer(s, 0, 1)}, device_id_type=MESH,
        )

    first = group(st, r1, TM - 1, s1, q1)
    asks = group(nbs, rnb, HOLD - 1, sn, qn)
    second = group(r2, r2, HOLD - 1, s2, q2)
    third = group(fin, fin, TM - 1, s3, q3)
    early_x = group(xs, ex, HOLD - 1, sx, qx)
    early_a = group(ags, ea, HOLD - 1, sa, qa)
    rows_out = group(send, o_ref, (HOLD - 1) * (CAP - 1), ss, qs)

    per = B // CHUNKS
    loads = [
        pltpu.make_async_copy(fact_hbm.at[pl.ds(k * per, per)], facts.at[pl.ds(k * per, per)], lsem.at[k])
        for k in range(CHUNKS)
    ]
    rest = [
        pltpu.make_async_copy(wself_hbm, w1.at[pl.ds(0, D)], lsem.at[CHUNKS]),
        pltpu.make_async_copy(wnbr_hbm, w1.at[pl.ds(D, D)], lsem.at[CHUNKS + 1]),
        pltpu.make_async_copy(wmid_hbm, wmid, lsem.at[CHUNKS + 2]),
        pltpu.make_async_copy(wout_hbm, wout, lsem.at[CHUNKS + 3]),
        pltpu.make_async_copy(ent_hbm, ent, lsem.at[CHUNKS + 4]),
    ]
    tables = [
        pltpu.make_async_copy(own_hbm, own_v, tsem.at[0]),
        pltpu.make_async_copy(cnt_hbm, cnt_v, tsem.at[1]),
        pltpu.make_async_copy(cnt1_hbm, cnt_s, tsem.at[2]),
        pltpu.make_async_copy(nb_hbm, nb_v, tsem.at[3]),
        pltpu.make_async_copy(gain_hbm, gain_v, tsem.at[4]),
        pltpu.make_async_copy(bias_hbm, bias_v, tsem.at[5]),
    ]
    for cp in tables + loads:
        cp.start()

    bar = pltpu.get_barrier_semaphore()
    for i in range(1, TM):
        pl.semaphore_signal(bar, inc=1, device_id={"tm": times[i]}, device_id_type=MESH)
    for d in range(1, HOLD):
        pl.semaphore_signal(bar, inc=1, device_id={"hash": near[d]}, device_id_type=MESH)

    for cp in rest:
        cp.start()
    for cp in tables:
        cp.wait()

    hot = (lax.broadcasted_iota(jnp.int32, (HOLD, B), 0) == own_v[...]).astype(F32)
    upper = (
        lax.broadcasted_iota(jnp.int32, (B, B), 0) <= lax.broadcasted_iota(jnp.int32, (B, B), 1)
    ).astype(BF16)
    order = jnp.dot(hot.astype(BF16), upper, preferred_element_type=F32)
    cnt = cnt_v[...].astype(F32)
    blk = lax.broadcasted_iota(jnp.int32, (HOLD, B), 1).astype(F32)
    lane = lax.broadcasted_iota(jnp.int32, (HOLD, 128), 1)
    tab = jnp.zeros((HOLD, 128), F32)
    for c in range(CAP):
        sel = jnp.where(order == float(c + 1), hot, 0.0)
        tab = jnp.where(lane == c, jnp.sum(sel * blk, axis=1, keepdims=True), tab)
        tab = jnp.where(lane == 16 + c, jnp.sum(sel * cnt, axis=1, keepdims=True), tab)
    tab_v[...] = tab.astype(jnp.int32)
    tab_copy = pltpu.make_async_copy(tab_v, tab_s, lsem.at[CHUNKS + 5])
    tab_copy.start()

    wide[...] = jnp.zeros_like(wide)
    for q in range(2 * CAP):
        wide[q : q + 1, 0:HOLD] = nb_v[q]
    note = jnp.where(lane < 16, wide[...].T[0:HOLD, :], tab_v[...])
    for j in range(HOLD):
        nbs[j] = note[j : j + 1, :]

    row = lax.broadcasted_iota(jnp.int32, (R, D), 0)
    for k in range(CHUNKS):
        loads[k].wait()

        def stat(i, carry):
            for j in range(2):
                b = k * per + i * 2 + j
                x = jnp.where(row < cnt_s[b], facts[b].astype(F32), 0.0)
                bs[pl.ds(b, 1), :] = jnp.sum(x, axis=0, keepdims=True)
                bq[pl.ds(b, 1), :] = jnp.sum(x * x, axis=0, keepdims=True)
            return carry

        lax.fori_loop(0, per // 2, stat, 0)
    sums = jnp.dot(hot, bs[...], preferred_element_type=F32, precision=lax.Precision.HIGHEST)
    squares = jnp.dot(hot, bq[...], preferred_element_type=F32, precision=lax.Precision.HIGHEST)
    live = jnp.broadcast_to(jnp.sum(hot * cnt, axis=1, keepdims=True), (HOLD, 128))
    st[...] = jnp.zeros_like(st)
    fin[...] = jnp.zeros_like(fin)
    for h in range(HOLD):
        base = 3 * (h % 2)
        st[h // 2, base : base + 1, :] = sums[h : h + 1, :]
        st[h // 2, base + 1 : base + 2, :] = squares[h : h + 1, :]
        st[h // 2, base + 2 : base + 3, :] = live[h : h + 1, :]

    tab_copy.wait()
    for d in range(HOLD):
        p = near[d]
        x = facts[jnp.clip(tab_s[p, CAP - 1], 0, B - 1)]
        if d:
            xs[p] = x
        else:
            ex[s] = x

    pl.semaphore_wait(bar, TM - 1 + HOLD - 1)

    for i in range(1, TM):
        p = times[i]
        pltpu.make_async_remote_copy(
            src_ref=st.at[p], dst_ref=r1.at[t], send_sem=s1.at[0], recv_sem=q1.at[0],
            device_id={"tm": p}, device_id_type=MESH,
        ).start()
    for d in range(1, HOLD):
        p = near[d]
        pltpu.make_async_remote_copy(
            src_ref=nbs.at[p], dst_ref=rnb.at[s], send_sem=sn.at[0], recv_sem=qn.at[0],
            device_id={"hash": p}, device_id_type=MESH,
        ).start()
    for d in range(1, HOLD):
        p = near[d]
        pltpu.make_async_remote_copy(
            src_ref=xs.at[p], dst_ref=ex.at[s], send_sem=sx.at[0], recv_sem=qx.at[0],
            device_id={"hash": p}, device_id_type=MESH,
        ).start()
    rnb[s] = nbs[s]
    r1[t] = st[t]
    first.wait_recv()
    r2[s] = jnp.sum(r1[...], axis=0)
    for d in range(1, HOLD):
        p = near[d]
        pltpu.make_async_remote_copy(
            src_ref=r2.at[s], dst_ref=r2.at[s], send_sem=s2.at[0], recv_sem=q2.at[0],
            device_id={"hash": p}, device_id_type=MESH,
        ).start()
    asks.wait_recv()
    for h in range(HOLD):
        nbt_v[h : h + 1, :] = rnb[h]
    nb_copy = pltpu.make_async_copy(nbt_v, nb_s, lsem.at[CHUNKS + 6])
    nb_copy.start()
    second.wait_recv()
    total = jnp.sum(r2[...], axis=0)
    for k in range(2):
        mean = total[3 * k : 3 * k + 1, :] / total[3 * k + 2 : 3 * k + 3, :]
        var = total[3 * k + 1 : 3 * k + 2, :] / total[3 * k + 2 : 3 * k + 3, :] - mean * mean
        fin[t, 2 * k : 2 * k + 1, :] = mean
        fin[t, 2 * k + 1 : 2 * k + 2, :] = lax.rsqrt(var + EPS) * gain_v[...]
    for i in range(1, TM):
        p = times[i]
        pltpu.make_async_remote_copy(
            src_ref=fin.at[t], dst_ref=fin.at[t], send_sem=s3.at[0], recv_sem=q3.at[0],
            device_id={"tm": p}, device_id_type=MESH,
        ).start()
    for cp in rest:
        cp.wait()
    nb_copy.wait()

    def agg_of(p, c):
        e = ent[nb_s[p, 2 * c]].astype(F32) + ent[nb_s[p, 2 * c + 1]].astype(F32)
        return (e * 0.5).astype(BF16)

    for d in range(HOLD):
        p = near[d]
        if d:
            ags[p] = agg_of(p, CAP - 1)
            pltpu.make_async_remote_copy(
                    src_ref=ags.at[p], dst_ref=ea.at[s], send_sem=sa.at[0], recv_sem=qa.at[0],
                    device_id={"hash": p}, device_id_type=MESH,
            ).start()
        else:
            ea[s] = agg_of(p, CAP - 1)
    third.wait_recv()
    for h in range(HOLD):
        mean_v[h : h + 1, :] = fin[h // 2, 2 * (h % 2) : 2 * (h % 2) + 1, :]
        scale_v[h : h + 1, :] = fin[h // 2, 2 * (h % 2) + 1 : 2 * (h % 2) + 2, :]

    def copy_of(dz, dx, c):
        k = (dz * 4 + dx) * CAP + c
        return pltpu.make_async_remote_copy(
            src_ref=send.at[k], dst_ref=o_ref.at[s * CAP + c], send_sem=ss.at[0], recv_sem=qs.at[0],
            device_id={"hash": peer(s, dz, dx)}, device_id_type=MESH,
        )

    def own_copy(c):
        return pltpu.make_async_copy(send.at[c], o_ref.at[s * CAP + c], lsem.at[CHUNKS + 7])

    def norm_of(x, p):
        x = (x.astype(F32) - mean_v[pl.ds(p, 1), :]) * scale_v[pl.ds(p, 1), :]
        return x.astype(BF16)

    def layers():
        h1 = jnp.dot(in1[...], w1[...], preferred_element_type=F32) + bias_v[...]
        h1 = jnp.maximum(h1, 0.0).astype(BF16)
        h2 = jnp.dot(h1, wmid[...], preferred_element_type=F32)
        h2 = jnp.maximum(h2, 0.0).astype(BF16)
        return jnp.dot(h2, wout[...], preferred_element_type=F32)

    def step(n, carry):
        c, dz = lax.div(n, 4), lax.rem(n, 4)
        for dx in range(4):
            p = peer(s, dz, dx)
            in1[dx * R : (dx + 1) * R, 0:D] = norm_of(facts[jnp.clip(tab_s[p, c], 0, B - 1)], p)
            in1[dx * R : (dx + 1) * R, D : 2 * D] = agg_of(p, c)
        out = layers()
        for dx in range(4):
            p = peer(s, dz, dx)
            y = jnp.where(row < tab_s[p, 16 + c], out[dx * R : (dx + 1) * R, :], 0.0)
            send[(dz * 4 + dx) * CAP + c] = y.astype(BF16)
            if dx:
                copy_of(dz, dx, c).start()
            else:

                @pl.when(dz > 0)
                def _():
                    copy_of(dz, 0, c).start()

                @pl.when(dz == 0)
                def _():
                    own_copy(c).start()

        return carry

    lax.fori_loop(0, 4 * (CAP - 1), step, 0)

    early_x.wait_recv()
    early_a.wait_recv()

    def late_copy(k):
        return pltpu.make_async_copy(ea.at[k], o_ref.at[k * CAP + CAP - 1], lsem.at[CHUNKS + 8])

    def late(n, carry):
        for i in range(4):
            k = n * 4 + i
            in1[i * R : (i + 1) * R, 0:D] = norm_of(ex[k], s)
            in1[i * R : (i + 1) * R, D : 2 * D] = ea[k]
        out = layers()
        for i in range(4):
            k = n * 4 + i
            y = jnp.where(row < nb_s[k, 16 + CAP - 1], out[i * R : (i + 1) * R, :], 0.0)
            ea[k] = y.astype(BF16)
            late_copy(k).start()
        return carry

    lax.fori_loop(0, HOLD // 4, late, 0)

    for cp in (first, asks, second, third, early_x, early_a, rows_out):
        cp.wait_send()
    pltpu.make_async_copy(send.at[pl.ds(0, CAP - 1)], o_ref.at[pl.ds(0, CAP - 1)], lsem.at[CHUNKS + 7]).wait()
    pltpu.make_async_copy(ea, o_ref.at[pl.ds(0, HOLD)], lsem.at[CHUNKS + 8]).wait()
    rows_out.wait_recv()


def place(x_ref, o_ref, buf, rsem, wsem):
    per = HOLD * CAP // PIECES
    reads, writes = [], []
    for k in range(PIECES):
        part = pl.ds(k * per, per)
        reads.append(pltpu.make_async_copy(x_ref.at[part], buf.at[part], rsem.at[k]))
        writes.append(pltpu.make_async_copy(buf.at[part], o_ref.at[0, part], wsem.at[k]))
        reads[-1].start()
    for read, write in zip(reads, writes):
        read.wait()
        write.start()
    for write in writes:
        write.wait()


def body(fact_blocks, owners, row_counts, neighbours, entities, col_gain, w_self, w_nbr, mlp_bias, w_mid, w_out):
    hbm = pl.BlockSpec(memory_space=pl.ANY)
    dma = pltpu.SemaphoreType.DMA
    out = pl.pallas_call(
        kernel,
        out_shape=jax.ShapeDtypeStruct((HOLD * CAP, R, D), BF16),
        in_specs=[hbm] * 12,
        out_specs=hbm,
        scratch_shapes=[
            pltpu.VMEM((1, B), jnp.int32),
            pltpu.VMEM((1, B), jnp.int32),
            pltpu.SMEM((B,), jnp.int32),
            pltpu.VMEM((2 * CAP, 1, HOLD), jnp.int32),
            pltpu.VMEM((1, D), F32),
            pltpu.VMEM((1, HID), F32),
            pltpu.VMEM((B, R, D), BF16),
            pltpu.VMEM((64, R, D), BF16),
            pltpu.VMEM((2 * D, HID), BF16),
            pltpu.VMEM((HID, HID), BF16),
            pltpu.VMEM((HID, D), BF16),
            pltpu.VMEM((B, D), F32),
            pltpu.VMEM((B, D), F32),
            pltpu.VMEM((TM, 8, 128), F32),
            pltpu.VMEM((TM, 8, 128), F32),
            pltpu.VMEM((HOLD, 8, 128), F32),
            pltpu.VMEM((TM, 8, 128), F32),
            pltpu.VMEM((HOLD, 1, 128), jnp.int32),
            pltpu.VMEM((HOLD, 1, 128), jnp.int32),
            pltpu.VMEM((128, 128), jnp.int32),
            pltpu.VMEM((HOLD, 128), jnp.int32),
            pltpu.VMEM((HOLD, 128), jnp.int32),
            pltpu.SMEM((HOLD, 128), jnp.int32),
            pltpu.SMEM((HOLD, 128), jnp.int32),
            pltpu.VMEM((HOLD, D), F32),
            pltpu.VMEM((HOLD, D), F32),
            pltpu.VMEM((4 * R, 2 * D), BF16),
            pltpu.VMEM((HOLD * CAP, R, D), BF16),
            pltpu.VMEM((HOLD, R, D), BF16),
            pltpu.VMEM((HOLD, R, D), BF16),
            pltpu.VMEM((HOLD, R, D), BF16),
            pltpu.VMEM((HOLD, R, D), BF16),
            dma((CHUNKS + 9,)),
            *[dma((1,))] * 14,
            dma((6,)),
        ],
        compiler_params=pltpu.CompilerParams(
            collective_id=0, has_side_effects=True, vmem_limit_bytes=60 << 20
        ),
        cost_estimate=pl.CostEstimate(flops=12 * 10**9, bytes_accessed=10 * 2**20, transcendentals=0),
    )(
        fact_blocks,
        owners.reshape(1, B),
        row_counts.reshape(1, B),
        row_counts,
        neighbours.transpose(2, 0, 1),
        entities,
        col_gain.reshape(1, D),
        w_self,
        w_nbr,
        mlp_bias.reshape(1, HID),
        w_mid,
        w_out,
    )
    return pl.pallas_call(
        place,
        out_shape=jax.ShapeDtypeStruct((1, HOLD * CAP, R, D), BF16),
        in_specs=[hbm],
        out_specs=hbm,
        scratch_shapes=[pltpu.VMEM((HOLD * CAP, R, D), BF16), dma((PIECES,)), dma((PIECES,))],
        compiler_params=pltpu.CompilerParams(vmem_limit_bytes=60 << 20),
    )(out)


def solution(mesh):
    return jax.shard_map(
        body,
        mesh=mesh,
        in_specs=(
            P(("tm", "hash"), None, None),
            P(("tm", "hash")),
            P(("tm", "hash")),
            P(("tm", "hash"), None, None),
            P("hash", None, None),
            P(),
            P(),
            P(),
            P(),
            P(),
            P(),
        ),
        out_specs=P(("tm", "hash"), None, None, None),
        check_vma=False,
    )
```

```python
import functools

import jax
import jax.numpy as jnp
from jax import lax
from jax.experimental import pallas as pl
from jax.experimental.pallas import tpu as pltpu
from jax.sharding import PartitionSpec as P

MESH = pl.DeviceIdType.MESH
HOLD = 16
TM = 8
CAP = 6
B = 48
R = 128
D = 128
HID = 512
EPS = 1e-05
CHUNKS = 4
PIECES = 8
F32 = jnp.float32
BF16 = jnp.bfloat16


def peer(s, dz, dx):
    return lax.rem(lax.div(s, 4) + dz, 4) * 4 + lax.rem(lax.rem(s, 4) + dx, 4)


def kernel(
    fact_hbm, own_hbm, cnt_hbm, cnt1_hbm, nb_hbm, ent_hbm, gain_hbm, wself_hbm, wnbr_hbm, bias_hbm, wmid_hbm, wout_hbm,
    o_ref,
    own_v, cnt_v, cnt_s, nb_v, gain_v, bias_v, facts, ent, w1, wmid, wout, bs, bq, st, r1, r2, fin, nbs, rnb, wide, tab_v, nbt_v, tab_s, nb_s, mean_v, scale_v,
    in1, send, xs, ags, ex, ea, lsem, s1, q1, s2, q2, s3, q3, sn, qn, sx, qx, sa, qa, ss, qs, tsem,
):
    t = lax.axis_index("tm")
    s = lax.axis_index("hash")

    zs = [lax.rem(lax.div(s, 4) + d, 4) * 4 for d in range(4)]
    xc = [lax.rem(lax.rem(s, 4) + d, 4) for d in range(4)]
    near = [s] + [zs[d // 4] + xc[d % 4] for d in (10, 6, 9, 14, 11, 2, 8, 5, 7, 13, 15, 1, 4, 3, 12)]
    times = [t] + [lax.rem(t + i, TM) for i in range(1, TM)]

    def group(src, dst, n, send_sem, recv_sem):
        return pltpu.make_async_remote_copy(
            src_ref=src.at[pl.ds(0, n)], dst_ref=dst.at[pl.ds(0, n)], send_sem=send_sem.at[0],
            recv_sem=recv_sem.at[0], device_id={"hash": peer(s, 0, 1)}, device_id_type=MESH,
        )

    first = group(st, r1, TM - 1, s1, q1)
    asks = group(nbs, rnb, HOLD - 1, sn, qn)
    second = group(r2, r2, HOLD - 1, s2, q2)
    third = group(fin, fin, TM - 1, s3, q3)
    early_x = group(xs, ex, HOLD - 1, sx, qx)
    early_a = group(ags, ea, HOLD - 1, sa, qa)
    rows_out = group(send, o_ref, (HOLD - 1) * (CAP - 1), ss, qs)

    per = B // CHUNKS
    loads = [
        pltpu.make_async_copy(fact_hbm.at[pl.ds(k * per, per)], facts.at[pl.ds(k * per, per)], lsem.at[k])
        for k in range(CHUNKS)
    ]
    rest = [
        pltpu.make_async_copy(wself_hbm, w1.at[pl.ds(0, D)], lsem.at[CHUNKS]),
        pltpu.make_async_copy(wnbr_hbm, w1.at[pl.ds(D, D)], lsem.at[CHUNKS + 1]),
        pltpu.make_async_copy(wmid_hbm, wmid, lsem.at[CHUNKS + 2]),
        pltpu.make_async_copy(wout_hbm, wout, lsem.at[CHUNKS + 3]),
        pltpu.make_async_copy(ent_hbm, ent, lsem.at[CHUNKS + 4]),
    ]
    tables = [
        pltpu.make_async_copy(own_hbm, own_v, tsem.at[0]),
        pltpu.make_async_copy(cnt_hbm, cnt_v, tsem.at[1]),
        pltpu.make_async_copy(cnt1_hbm, cnt_s, tsem.at[2]),
        pltpu.make_async_copy(nb_hbm, nb_v, tsem.at[3]),
        pltpu.make_async_copy(gain_hbm, gain_v, tsem.at[4]),
        pltpu.make_async_copy(bias_hbm, bias_v, tsem.at[5]),
    ]
    for cp in tables + loads:
        cp.start()

    bar = pltpu.get_barrier_semaphore()
    for i in range(1, TM):
        pl.semaphore_signal(bar, inc=1, device_id={"tm": times[i]}, device_id_type=MESH)
    for d in range(1, HOLD):
        pl.semaphore_signal(bar, inc=1, device_id={"hash": near[d]}, device_id_type=MESH)

    for cp in rest:
        cp.start()
    for cp in tables:
        cp.wait()

    hot = (lax.broadcasted_iota(jnp.int32, (HOLD, B), 0) == own_v[...]).astype(F32)
    upper = (
        lax.broadcasted_iota(jnp.int32, (B, B), 0) <= lax.broadcasted_iota(jnp.int32, (B, B), 1)
    ).astype(BF16)
    order = jnp.dot(hot.astype(BF16), upper, preferred_element_type=F32)
    cnt = cnt_v[...].astype(F32)
    blk = lax.broadcasted_iota(jnp.int32, (HOLD, B), 1).astype(F32)
    lane = lax.broadcasted_iota(jnp.int32, (HOLD, 128), 1)
    tab = jnp.zeros((HOLD, 128), F32)
    for c in range(CAP):
        sel = jnp.where(order == float(c + 1), hot, 0.0)
        tab = jnp.where(lane == c, jnp.sum(sel * blk, axis=1, keepdims=True), tab)
        tab = jnp.where(lane == 16 + c, jnp.sum(sel * cnt, axis=1, keepdims=True), tab)
    tab_v[...] = tab.astype(jnp.int32)
    tab_copy = pltpu.make_async_copy(tab_v, tab_s, lsem.at[CHUNKS + 5])
    tab_copy.start()

    wide[...] = jnp.zeros_like(wide)
    for q in range(2 * CAP):
        wide[q : q + 1, 0:HOLD] = nb_v[q]
    note = jnp.where(lane < 16, wide[...].T[0:HOLD, :], tab_v[...])
    for j in range(HOLD):
        nbs[j] = note[j : j + 1, :]

    row = lax.broadcasted_iota(jnp.int32, (R, D), 0)
    for k in range(CHUNKS):
        loads[k].wait()

        def stat(i, carry):
            for j in range(2):
                b = k * per + i * 2 + j
                x = jnp.where(row < cnt_s[b], facts[b].astype(F32), 0.0)
                bs[pl.ds(b, 1), :] = jnp.sum(x, axis=0, keepdims=True)
                bq[pl.ds(b, 1), :] = jnp.sum(x * x, axis=0, keepdims=True)
            return carry

        lax.fori_loop(0, per // 2, stat, 0)
    sums = jnp.dot(hot, bs[...], preferred_element_type=F32, precision=lax.Precision.HIGHEST)
    squares = jnp.dot(hot, bq[...], preferred_element_type=F32, precision=lax.Precision.HIGHEST)
    live = jnp.broadcast_to(jnp.sum(hot * cnt, axis=1, keepdims=True), (HOLD, 128))
    st[...] = jnp.zeros_like(st)
    fin[...] = jnp.zeros_like(fin)
    for h in range(HOLD):
        base = 3 * (h % 2)
        st[h // 2, base : base + 1, :] = sums[h : h + 1, :]
        st[h // 2, base + 1 : base + 2, :] = squares[h : h + 1, :]
        st[h // 2, base + 2 : base + 3, :] = live[h : h + 1, :]

    tab_copy.wait()
    for d in range(HOLD):
        p = near[d]
        x = facts[jnp.clip(tab_s[p, CAP - 1], 0, B - 1)]
        if d:
            xs[p] = x
        else:
            ex[s] = x

    pl.semaphore_wait(bar, TM - 1 + HOLD - 1)

    for i in range(1, TM):
        p = times[i]
        pltpu.make_async_remote_copy(
            src_ref=st.at[p], dst_ref=r1.at[t], send_sem=s1.at[0], recv_sem=q1.at[0],
            device_id={"tm": p}, device_id_type=MESH,
        ).start()
    for d in range(1, HOLD):
        p = near[d]
        pltpu.make_async_remote_copy(
            src_ref=nbs.at[p], dst_ref=rnb.at[s], send_sem=sn.at[0], recv_sem=qn.at[0],
            device_id={"hash": p}, device_id_type=MESH,
        ).start()
    for d in range(1, HOLD):
        p = near[d]
        pltpu.make_async_remote_copy(
            src_ref=xs.at[p], dst_ref=ex.at[s], send_sem=sx.at[0], recv_sem=qx.at[0],
            device_id={"hash": p}, device_id_type=MESH,
        ).start()
    rnb[s] = nbs[s]
    r1[t] = st[t]
    first.wait_recv()
    r2[s] = jnp.sum(r1[...], axis=0)
    for d in range(1, HOLD):
        p = near[d]
        pltpu.make_async_remote_copy(
            src_ref=r2.at[s], dst_ref=r2.at[s], send_sem=s2.at[0], recv_sem=q2.at[0],
            device_id={"hash": p}, device_id_type=MESH,
        ).start()
    asks.wait_recv()
    for h in range(HOLD):
        nbt_v[h : h + 1, :] = rnb[h]
    nb_copy = pltpu.make_async_copy(nbt_v, nb_s, lsem.at[CHUNKS + 6])
    nb_copy.start()
    second.wait_recv()
    total = jnp.sum(r2[...], axis=0)
    for k in range(2):
        mean = total[3 * k : 3 * k + 1, :] / total[3 * k + 2 : 3 * k + 3, :]
        var = total[3 * k + 1 : 3 * k + 2, :] / total[3 * k + 2 : 3 * k + 3, :] - mean * mean
        fin[t, 2 * k : 2 * k + 1, :] = mean
        fin[t, 2 * k + 1 : 2 * k + 2, :] = lax.rsqrt(var + EPS) * gain_v[...]
    for i in range(1, TM):
        p = times[i]
        pltpu.make_async_remote_copy(
            src_ref=fin.at[t], dst_ref=fin.at[t], send_sem=s3.at[0], recv_sem=q3.at[0],
            device_id={"tm": p}, device_id_type=MESH,
        ).start()
    for cp in rest:
        cp.wait()
    nb_copy.wait()

    def agg_of(p, c):
        e = ent[nb_s[p, 2 * c]].astype(F32) + ent[nb_s[p, 2 * c + 1]].astype(F32)
        return (e * 0.5).astype(BF16)

    for d in range(HOLD):
        p = near[d]
        if d:
            ags[p] = agg_of(p, CAP - 1)
            pltpu.make_async_remote_copy(
                    src_ref=ags.at[p], dst_ref=ea.at[s], send_sem=sa.at[0], recv_sem=qa.at[0],
                    device_id={"hash": p}, device_id_type=MESH,
            ).start()
        else:
            ea[s] = agg_of(p, CAP - 1)
    third.wait_recv()
    for h in range(HOLD):
        mean_v[h : h + 1, :] = fin[h // 2, 2 * (h % 2) : 2 * (h % 2) + 1, :]
        scale_v[h : h + 1, :] = fin[h // 2, 2 * (h % 2) + 1 : 2 * (h % 2) + 2, :]

    def copy_of(dz, dx, c):
        k = (dz * 4 + dx) * CAP + c
        return pltpu.make_async_remote_copy(
            src_ref=send.at[k], dst_ref=o_ref.at[s * CAP + c], send_sem=ss.at[0], recv_sem=qs.at[0],
            device_id={"hash": peer(s, dz, dx)}, device_id_type=MESH,
        )

    def own_copy(c):
        return pltpu.make_async_copy(send.at[c], o_ref.at[s * CAP + c], lsem.at[CHUNKS + 7])

    def norm_of(x, p):
        x = (x.astype(F32) - mean_v[pl.ds(p, 1), :]) * scale_v[pl.ds(p, 1), :]
        return x.astype(BF16)

    def layers():
        h1 = jnp.dot(in1[...], w1[...], preferred_element_type=F32) + bias_v[...]
        h1 = jnp.maximum(h1, 0.0).astype(BF16)
        h2 = jnp.dot(h1, wmid[...], preferred_element_type=F32)
        h2 = jnp.maximum(h2, 0.0).astype(BF16)
        return jnp.dot(h2, wout[...], preferred_element_type=F32)

    def step(n, carry):
        c, dz = lax.div(n, 4), lax.rem(n + 2, 4)
        for dx in range(4):
            p = peer(s, dz, dx)
            in1[dx * R : (dx + 1) * R, 0:D] = norm_of(facts[jnp.clip(tab_s[p, c], 0, B - 1)], p)
            in1[dx * R : (dx + 1) * R, D : 2 * D] = agg_of(p, c)
        out = layers()
        for dx in range(4):
            p = peer(s, dz, dx)
            y = jnp.where(row < tab_s[p, 16 + c], out[dx * R : (dx + 1) * R, :], 0.0)
            send[(dz * 4 + dx) * CAP + c] = y.astype(BF16)
            if dx:
                copy_of(dz, dx, c).start()
            else:

                @pl.when(dz > 0)
                def _():
                    copy_of(dz, 0, c).start()

                @pl.when(dz == 0)
                def _():
                    own_copy(c).start()

        return carry

    lax.fori_loop(0, 4 * (CAP - 1), step, 0)

    early_x.wait_recv()
    early_a.wait_recv()

    def late_copy(k):
        return pltpu.make_async_copy(ea.at[k], o_ref.at[k * CAP + CAP - 1], lsem.at[CHUNKS + 8])

    def late(n, carry):
        for i in range(4):
            k = n * 4 + i
            in1[i * R : (i + 1) * R, 0:D] = norm_of(ex[k], s)
            in1[i * R : (i + 1) * R, D : 2 * D] = ea[k]
        out = layers()
        for i in range(4):
            k = n * 4 + i
            y = jnp.where(row < nb_s[k, 16 + CAP - 1], out[i * R : (i + 1) * R, :], 0.0)
            ea[k] = y.astype(BF16)
            late_copy(k).start()
        return carry

    lax.fori_loop(0, HOLD // 4, late, 0)

    for cp in (first, asks, second, third, early_x, early_a, rows_out):
        cp.wait_send()
    pltpu.make_async_copy(send.at[pl.ds(0, CAP - 1)], o_ref.at[pl.ds(0, CAP - 1)], lsem.at[CHUNKS + 7]).wait()
    pltpu.make_async_copy(ea, o_ref.at[pl.ds(0, HOLD)], lsem.at[CHUNKS + 8]).wait()
    rows_out.wait_recv()


def place(x_ref, o_ref, buf, rsem, wsem):
    per = HOLD * CAP // PIECES
    reads, writes = [], []
    for k in range(PIECES):
        part = pl.ds(k * per, per)
        reads.append(pltpu.make_async_copy(x_ref.at[part], buf.at[part], rsem.at[k]))
        writes.append(pltpu.make_async_copy(buf.at[part], o_ref.at[0, part], wsem.at[k]))
        reads[-1].start()
    for read, write in zip(reads, writes):
        read.wait()
        write.start()
    for write in writes:
        write.wait()


def body(fact_blocks, owners, row_counts, neighbours, entities, col_gain, w_self, w_nbr, mlp_bias, w_mid, w_out):
    hbm = pl.BlockSpec(memory_space=pl.ANY)
    dma = pltpu.SemaphoreType.DMA
    out = pl.pallas_call(
        kernel,
        out_shape=jax.ShapeDtypeStruct((HOLD * CAP, R, D), BF16),
        in_specs=[hbm] * 12,
        out_specs=hbm,
        scratch_shapes=[
            pltpu.VMEM((1, B), jnp.int32),
            pltpu.VMEM((1, B), jnp.int32),
            pltpu.SMEM((B,), jnp.int32),
            pltpu.VMEM((2 * CAP, 1, HOLD), jnp.int32),
            pltpu.VMEM((1, D), F32),
            pltpu.VMEM((1, HID), F32),
            pltpu.VMEM((B, R, D), BF16),
            pltpu.VMEM((64, R, D), BF16),
            pltpu.VMEM((2 * D, HID), BF16),
            pltpu.VMEM((HID, HID), BF16),
            pltpu.VMEM((HID, D), BF16),
            pltpu.VMEM((B, D), F32),
            pltpu.VMEM((B, D), F32),
            pltpu.VMEM((TM, 8, 128), F32),
            pltpu.VMEM((TM, 8, 128), F32),
            pltpu.VMEM((HOLD, 8, 128), F32),
            pltpu.VMEM((TM, 8, 128), F32),
            pltpu.VMEM((HOLD, 1, 128), jnp.int32),
            pltpu.VMEM((HOLD, 1, 128), jnp.int32),
            pltpu.VMEM((128, 128), jnp.int32),
            pltpu.VMEM((HOLD, 128), jnp.int32),
            pltpu.VMEM((HOLD, 128), jnp.int32),
            pltpu.SMEM((HOLD, 128), jnp.int32),
            pltpu.SMEM((HOLD, 128), jnp.int32),
            pltpu.VMEM((HOLD, D), F32),
            pltpu.VMEM((HOLD, D), F32),
            pltpu.VMEM((4 * R, 2 * D), BF16),
            pltpu.VMEM((HOLD * CAP, R, D), BF16),
            pltpu.VMEM((HOLD, R, D), BF16),
            pltpu.VMEM((HOLD, R, D), BF16),
            pltpu.VMEM((HOLD, R, D), BF16),
            pltpu.VMEM((HOLD, R, D), BF16),
            dma((CHUNKS + 9,)),
            *[dma((1,))] * 14,
            dma((6,)),
        ],
        compiler_params=pltpu.CompilerParams(
            collective_id=0, has_side_effects=True, vmem_limit_bytes=60 << 20
        ),
        cost_estimate=pl.CostEstimate(flops=12 * 10**9, bytes_accessed=10 * 2**20, transcendentals=0),
    )(
        fact_blocks,
        owners.reshape(1, B),
        row_counts.reshape(1, B),
        row_counts,
        neighbours.transpose(2, 0, 1),
        entities,
        col_gain.reshape(1, D),
        w_self,
        w_nbr,
        mlp_bias.reshape(1, HID),
        w_mid,
        w_out,
    )
    return pl.pallas_call(
        place,
        out_shape=jax.ShapeDtypeStruct((1, HOLD * CAP, R, D), BF16),
        in_specs=[hbm],
        out_specs=hbm,
        scratch_shapes=[pltpu.VMEM((HOLD * CAP, R, D), BF16), dma((PIECES,)), dma((PIECES,))],
        compiler_params=pltpu.CompilerParams(vmem_limit_bytes=60 << 20),
    )(out)


def solution(mesh):
    return jax.shard_map(
        body,
        mesh=mesh,
        in_specs=(
            P(("tm", "hash"), None, None),
            P(("tm", "hash")),
            P(("tm", "hash")),
            P(("tm", "hash"), None, None),
            P("hash", None, None),
            P(),
            P(),
            P(),
            P(),
            P(),
            P(),
        ),
        out_specs=P(("tm", "hash"), None, None, None),
        check_vma=False,
    )
```

```python
import functools

import jax
import jax.numpy as jnp
from jax import lax
from jax.experimental import pallas as pl
from jax.experimental.pallas import tpu as pltpu
from jax.sharding import PartitionSpec as P

MESH = pl.DeviceIdType.MESH
HOLD = 16
TM = 8
CAP = 6
B = 48
R = 128
D = 128
HID = 512
EPS = 1e-05
CHUNKS = 4
PIECES = 8
F32 = jnp.float32
BF16 = jnp.bfloat16


def peer(s, dz, dx):
    return lax.rem(lax.div(s, 4) + dz, 4) * 4 + lax.rem(lax.rem(s, 4) + dx, 4)


def kernel(
    fact_hbm, own_hbm, cnt_hbm, cnt1_hbm, nb_hbm, ent_hbm, gain_hbm, wself_hbm, wnbr_hbm, bias_hbm, wmid_hbm, wout_hbm,
    o_ref,
    own_v, cnt_v, cnt_s, nb_v, gain_v, bias_v, facts, ent, w1, wmid, wout, bs, bq, st, r1, r2, fin, nbs, rnb, wide, tab_v, nbt_v, tab_s, nb_s, mean_v, scale_v,
    in1, send, xs, ags, ex, ea, lsem, s1, q1, s2, q2, s3, q3, sn, qn, sx, qx, sa, qa, ss, qs, tsem,
):
    t = lax.axis_index("tm")
    s = lax.axis_index("hash")

    zs = [lax.rem(lax.div(s, 4) + d, 4) * 4 for d in range(4)]
    xc = [lax.rem(lax.rem(s, 4) + d, 4) for d in range(4)]
    near = [s] + [zs[d // 4] + xc[d % 4] for d in (10, 6, 9, 14, 11, 2, 8, 5, 7, 13, 15, 1, 4, 3, 12)]
    times = [t] + [lax.rem(t + i, TM) for i in range(1, TM)]

    def group(src, dst, n, send_sem, recv_sem):
        return pltpu.make_async_remote_copy(
            src_ref=src.at[pl.ds(0, n)], dst_ref=dst.at[pl.ds(0, n)], send_sem=send_sem.at[0],
            recv_sem=recv_sem.at[0], device_id={"hash": peer(s, 0, 1)}, device_id_type=MESH,
        )

    first = group(st, r1, TM - 1, s1, q1)
    asks = group(nbs, rnb, HOLD - 1, sn, qn)
    second = group(r2, r2, HOLD - 1, s2, q2)
    third = group(fin, fin, TM - 1, s3, q3)
    early_x = group(xs, ex, HOLD - 1, sx, qx)
    early_a = group(ags, ea, HOLD - 1, sa, qa)
    rows_out = group(send, o_ref, (HOLD - 1) * (CAP - 1), ss, qs)

    per = B // CHUNKS
    loads = [
        pltpu.make_async_copy(fact_hbm.at[pl.ds(k * per, per)], facts.at[pl.ds(k * per, per)], lsem.at[k])
        for k in range(CHUNKS)
    ]
    rest = [
        pltpu.make_async_copy(wself_hbm, w1.at[pl.ds(0, D)], lsem.at[CHUNKS]),
        pltpu.make_async_copy(wnbr_hbm, w1.at[pl.ds(D, D)], lsem.at[CHUNKS + 1]),
        pltpu.make_async_copy(wmid_hbm, wmid, lsem.at[CHUNKS + 2]),
        pltpu.make_async_copy(wout_hbm, wout, lsem.at[CHUNKS + 3]),
        pltpu.make_async_copy(ent_hbm, ent, lsem.at[CHUNKS + 4]),
    ]
    tables = [
        pltpu.make_async_copy(own_hbm, own_v, tsem.at[0]),
        pltpu.make_async_copy(cnt_hbm, cnt_v, tsem.at[1]),
        pltpu.make_async_copy(cnt1_hbm, cnt_s, tsem.at[2]),
        pltpu.make_async_copy(nb_hbm, nb_v, tsem.at[3]),
        pltpu.make_async_copy(gain_hbm, gain_v, tsem.at[4]),
        pltpu.make_async_copy(bias_hbm, bias_v, tsem.at[5]),
    ]
    for cp in tables + loads:
        cp.start()

    bar = pltpu.get_barrier_semaphore()
    for i in range(1, TM):
        pl.semaphore_signal(bar, inc=1, device_id={"tm": times[i]}, device_id_type=MESH)
    for d in range(1, HOLD):
        pl.semaphore_signal(bar, inc=1, device_id={"hash": near[d]}, device_id_type=MESH)

    for cp in rest:
        cp.start()
    for cp in tables:
        cp.wait()

    hot = (lax.broadcasted_iota(jnp.int32, (HOLD, B), 0) == own_v[...]).astype(F32)
    upper = (
        lax.broadcasted_iota(jnp.int32, (B, B), 0) <= lax.broadcasted_iota(jnp.int32, (B, B), 1)
    ).astype(BF16)
    order = jnp.dot(hot.astype(BF16), upper, preferred_element_type=F32)
    cnt = cnt_v[...].astype(F32)
    blk = lax.broadcasted_iota(jnp.int32, (HOLD, B), 1).astype(F32)
    lane = lax.broadcasted_iota(jnp.int32, (HOLD, 128), 1)
    tab = jnp.zeros((HOLD, 128), F32)
    for c in range(CAP):
        sel = jnp.where(order == float(c + 1), hot, 0.0)
        tab = jnp.where(lane == c, jnp.sum(sel * blk, axis=1, keepdims=True), tab)
        tab = jnp.where(lane == 16 + c, jnp.sum(sel * cnt, axis=1, keepdims=True), tab)
    tab_v[...] = tab.astype(jnp.int32)
    tab_copy = pltpu.make_async_copy(tab_v, tab_s, lsem.at[CHUNKS + 5])
    tab_copy.start()

    wide[...] = jnp.zeros_like(wide)
    for q in range(2 * CAP):
        wide[q : q + 1, 0:HOLD] = nb_v[q]
    note = jnp.where(lane < 16, wide[...].T[0:HOLD, :], tab_v[...])
    for j in range(HOLD):
        nbs[j] = note[j : j + 1, :]

    row = lax.broadcasted_iota(jnp.int32, (R, D), 0)
    for k in range(CHUNKS):
        loads[k].wait()

        def stat(i, carry):
            for j in range(2):
                b = k * per + i * 2 + j
                x = jnp.where(row < cnt_s[b], facts[b].astype(F32), 0.0)
                bs[pl.ds(b, 1), :] = jnp.sum(x, axis=0, keepdims=True)
                bq[pl.ds(b, 1), :] = jnp.sum(x * x, axis=0, keepdims=True)
            return carry

        lax.fori_loop(0, per // 2, stat, 0)
    sums = jnp.dot(hot, bs[...], preferred_element_type=F32, precision=lax.Precision.HIGHEST)
    squares = jnp.dot(hot, bq[...], preferred_element_type=F32, precision=lax.Precision.HIGHEST)
    live = jnp.broadcast_to(jnp.sum(hot * cnt, axis=1, keepdims=True), (HOLD, 128))
    st[...] = jnp.zeros_like(st)
    fin[...] = jnp.zeros_like(fin)
    for h in range(HOLD):
        base = 3 * (h % 2)
        st[h // 2, base : base + 1, :] = sums[h : h + 1, :]
        st[h // 2, base + 1 : base + 2, :] = squares[h : h + 1, :]
        st[h // 2, base + 2 : base + 3, :] = live[h : h + 1, :]

    tab_copy.wait()
    for d in range(HOLD):
        p = near[d]
        x = facts[jnp.clip(tab_s[p, CAP - 1], 0, B - 1)]
        if d:
            xs[p] = x
        else:
            ex[s] = x

    pl.semaphore_wait(bar, TM - 1 + HOLD - 1)

    for i in range(1, TM):
        p = times[i]
        pltpu.make_async_remote_copy(
            src_ref=st.at[p], dst_ref=r1.at[t], send_sem=s1.at[0], recv_sem=q1.at[0],
            device_id={"tm": p}, device_id_type=MESH,
        ).start()
    for d in range(1, HOLD):
        p = near[d]
        pltpu.make_async_remote_copy(
            src_ref=nbs.at[p], dst_ref=rnb.at[s], send_sem=sn.at[0], recv_sem=qn.at[0],
            device_id={"hash": p}, device_id_type=MESH,
        ).start()
    for d in range(1, HOLD):
        p = near[d]
        pltpu.make_async_remote_copy(
            src_ref=xs.at[p], dst_ref=ex.at[s], send_sem=sx.at[0], recv_sem=qx.at[0],
            device_id={"hash": p}, device_id_type=MESH,
        ).start()
    rnb[s] = nbs[s]
    r1[t] = st[t]
    first.wait_recv()
    r2[s] = jnp.sum(r1[...], axis=0)
    for d in range(1, HOLD):
        p = near[d]
        pltpu.make_async_remote_copy(
            src_ref=r2.at[s], dst_ref=r2.at[s], send_sem=s2.at[0], recv_sem=q2.at[0],
            device_id={"hash": p}, device_id_type=MESH,
        ).start()
    asks.wait_recv()
    for h in range(HOLD):
        nbt_v[h : h + 1, :] = rnb[h]
    nb_copy = pltpu.make_async_copy(nbt_v, nb_s, lsem.at[CHUNKS + 6])
    nb_copy.start()
    second.wait_recv()
    total = jnp.sum(r2[...], axis=0)
    for k in range(2):
        mean = total[3 * k : 3 * k + 1, :] / total[3 * k + 2 : 3 * k + 3, :]
        var = total[3 * k + 1 : 3 * k + 2, :] / total[3 * k + 2 : 3 * k + 3, :] - mean * mean
        fin[t, 2 * k : 2 * k + 1, :] = mean
        fin[t, 2 * k + 1 : 2 * k + 2, :] = lax.rsqrt(var + EPS) * gain_v[...]
    for i in range(1, TM):
        p = times[i]
        pltpu.make_async_remote_copy(
            src_ref=fin.at[t], dst_ref=fin.at[t], send_sem=s3.at[0], recv_sem=q3.at[0],
            device_id={"tm": p}, device_id_type=MESH,
        ).start()
    for cp in rest:
        cp.wait()
    nb_copy.wait()

    def agg_of(p, c):
        e = ent[nb_s[p, 2 * c]].astype(F32) + ent[nb_s[p, 2 * c + 1]].astype(F32)
        return (e * 0.5).astype(BF16)

    for d in range(HOLD):
        p = near[d]
        if d:
            ags[p] = agg_of(p, CAP - 1)
            pltpu.make_async_remote_copy(
                    src_ref=ags.at[p], dst_ref=ea.at[s], send_sem=sa.at[0], recv_sem=qa.at[0],
                    device_id={"hash": p}, device_id_type=MESH,
            ).start()
        else:
            ea[s] = agg_of(p, CAP - 1)
    third.wait_recv()
    for h in range(HOLD):
        mean_v[h : h + 1, :] = fin[h // 2, 2 * (h % 2) : 2 * (h % 2) + 1, :]
        scale_v[h : h + 1, :] = fin[h // 2, 2 * (h % 2) + 1 : 2 * (h % 2) + 2, :]

    def copy_of(dz, dx, c, half):
        k = (dz * 4 + dx) * CAP + c
        return pltpu.make_async_remote_copy(
            src_ref=send.at[k, pl.ds(half * (R // 2), R // 2)],
            dst_ref=o_ref.at[s * CAP + c, pl.ds(half * (R // 2), R // 2)], send_sem=ss.at[0], recv_sem=qs.at[0],
            device_id={"hash": peer(s, dz, dx)}, device_id_type=MESH,
        )

    def own_copy(c):
        return pltpu.make_async_copy(send.at[c], o_ref.at[s * CAP + c], lsem.at[CHUNKS + 7])

    def norm_of(x, p):
        x = (x.astype(F32) - mean_v[pl.ds(p, 1), :]) * scale_v[pl.ds(p, 1), :]
        return x.astype(BF16)

    def layers():
        h1 = jnp.dot(in1[...], w1[...], preferred_element_type=F32) + bias_v[...]
        h1 = jnp.maximum(h1, 0.0).astype(BF16)
        h2 = jnp.dot(h1, wmid[...], preferred_element_type=F32)
        h2 = jnp.maximum(h2, 0.0).astype(BF16)
        return jnp.dot(h2, wout[...], preferred_element_type=F32)

    def step(n, carry):
        c, dz = lax.div(n, 4), lax.rem(n, 4)
        for dx in range(4):
            p = peer(s, dz, dx)
            in1[dx * R : (dx + 1) * R, 0:D] = norm_of(facts[jnp.clip(tab_s[p, c], 0, B - 1)], p)
            in1[dx * R : (dx + 1) * R, D : 2 * D] = agg_of(p, c)
        out = layers()
        for dx in range(4):
            p = peer(s, dz, dx)
            y = jnp.where(row < tab_s[p, 16 + c], out[dx * R : (dx + 1) * R, :], 0.0)
            send[(dz * 4 + dx) * CAP + c] = y.astype(BF16)
            if dx:
                for half in range(2):
                    copy_of(dz, dx, c, half).start()
            else:

                @pl.when(dz > 0)
                def _():
                    for half in range(2):
                        copy_of(dz, 0, c, half).start()

                @pl.when(dz == 0)
                def _():
                    own_copy(c).start()

        return carry

    lax.fori_loop(0, 4 * (CAP - 1), step, 0)

    early_x.wait_recv()
    early_a.wait_recv()

    def late_copy(k):
        return pltpu.make_async_copy(ea.at[k], o_ref.at[k * CAP + CAP - 1], lsem.at[CHUNKS + 8])

    def late(n, carry):
        for i in range(4):
            k = n * 4 + i
            in1[i * R : (i + 1) * R, 0:D] = norm_of(ex[k], s)
            in1[i * R : (i + 1) * R, D : 2 * D] = ea[k]
        out = layers()
        for i in range(4):
            k = n * 4 + i
            y = jnp.where(row < nb_s[k, 16 + CAP - 1], out[i * R : (i + 1) * R, :], 0.0)
            ea[k] = y.astype(BF16)
            late_copy(k).start()
        return carry

    lax.fori_loop(0, HOLD // 4, late, 0)

    for cp in (first, asks, second, third, early_x, early_a, rows_out):
        cp.wait_send()
    pltpu.make_async_copy(send.at[pl.ds(0, CAP - 1)], o_ref.at[pl.ds(0, CAP - 1)], lsem.at[CHUNKS + 7]).wait()
    pltpu.make_async_copy(ea, o_ref.at[pl.ds(0, HOLD)], lsem.at[CHUNKS + 8]).wait()
    rows_out.wait_recv()


def place(x_ref, o_ref, buf, rsem, wsem):
    per = HOLD * CAP // PIECES
    reads, writes = [], []
    for k in range(PIECES):
        part = pl.ds(k * per, per)
        reads.append(pltpu.make_async_copy(x_ref.at[part], buf.at[part], rsem.at[k]))
        writes.append(pltpu.make_async_copy(buf.at[part], o_ref.at[0, part], wsem.at[k]))
        reads[-1].start()
    for read, write in zip(reads, writes):
        read.wait()
        write.start()
    for write in writes:
        write.wait()


def body(fact_blocks, owners, row_counts, neighbours, entities, col_gain, w_self, w_nbr, mlp_bias, w_mid, w_out):
    hbm = pl.BlockSpec(memory_space=pl.ANY)
    dma = pltpu.SemaphoreType.DMA
    out = pl.pallas_call(
        kernel,
        out_shape=jax.ShapeDtypeStruct((HOLD * CAP, R, D), BF16),
        in_specs=[hbm] * 12,
        out_specs=hbm,
        scratch_shapes=[
            pltpu.VMEM((1, B), jnp.int32),
            pltpu.VMEM((1, B), jnp.int32),
            pltpu.SMEM((B,), jnp.int32),
            pltpu.VMEM((2 * CAP, 1, HOLD), jnp.int32),
            pltpu.VMEM((1, D), F32),
            pltpu.VMEM((1, HID), F32),
            pltpu.VMEM((B, R, D), BF16),
            pltpu.VMEM((64, R, D), BF16),
            pltpu.VMEM((2 * D, HID), BF16),
            pltpu.VMEM((HID, HID), BF16),
            pltpu.VMEM((HID, D), BF16),
            pltpu.VMEM((B, D), F32),
            pltpu.VMEM((B, D), F32),
            pltpu.VMEM((TM, 8, 128), F32),
            pltpu.VMEM((TM, 8, 128), F32),
            pltpu.VMEM((HOLD, 8, 128), F32),
            pltpu.VMEM((TM, 8, 128), F32),
            pltpu.VMEM((HOLD, 1, 128), jnp.int32),
            pltpu.VMEM((HOLD, 1, 128), jnp.int32),
            pltpu.VMEM((128, 128), jnp.int32),
            pltpu.VMEM((HOLD, 128), jnp.int32),
            pltpu.VMEM((HOLD, 128), jnp.int32),
            pltpu.SMEM((HOLD, 128), jnp.int32),
            pltpu.SMEM((HOLD, 128), jnp.int32),
            pltpu.VMEM((HOLD, D), F32),
            pltpu.VMEM((HOLD, D), F32),
            pltpu.VMEM((4 * R, 2 * D), BF16),
            pltpu.VMEM((HOLD * CAP, R, D), BF16),
            pltpu.VMEM((HOLD, R, D), BF16),
            pltpu.VMEM((HOLD, R, D), BF16),
            pltpu.VMEM((HOLD, R, D), BF16),
            pltpu.VMEM((HOLD, R, D), BF16),
            dma((CHUNKS + 9,)),
            *[dma((1,))] * 14,
            dma((6,)),
        ],
        compiler_params=pltpu.CompilerParams(
            collective_id=0, has_side_effects=True, vmem_limit_bytes=60 << 20
        ),
        cost_estimate=pl.CostEstimate(flops=12 * 10**9, bytes_accessed=10 * 2**20, transcendentals=0),
    )(
        fact_blocks,
        owners.reshape(1, B),
        row_counts.reshape(1, B),
        row_counts,
        neighbours.transpose(2, 0, 1),
        entities,
        col_gain.reshape(1, D),
        w_self,
        w_nbr,
        mlp_bias.reshape(1, HID),
        w_mid,
        w_out,
    )
    return pl.pallas_call(
        place,
        out_shape=jax.ShapeDtypeStruct((1, HOLD * CAP, R, D), BF16),
        in_specs=[hbm],
        out_specs=hbm,
        scratch_shapes=[pltpu.VMEM((HOLD * CAP, R, D), BF16), dma((PIECES,)), dma((PIECES,))],
        compiler_params=pltpu.CompilerParams(vmem_limit_bytes=60 << 20),
    )(out)


def solution(mesh):
    return jax.shard_map(
        body,
        mesh=mesh,
        in_specs=(
            P(("tm", "hash"), None, None),
            P(("tm", "hash")),
            P(("tm", "hash")),
            P(("tm", "hash"), None, None),
            P("hash", None, None),
            P(),
            P(),
            P(),
            P(),
            P(),
            P(),
        ),
        out_specs=P(("tm", "hash"), None, None, None),
        check_vma=False,
    )
```
